32 devices in a mesh: rows: 8 (over z, y), panels: 4 (over x, core).
Axes of the slice: x: 2, y: 2, z: 4, core: 2. Of those that a mesh axis runs over, the one named last changes fastest.
Arguments:
- panel_left: float32 [8, 32, 64, 2048], P('rows', 'panels'), may hold values from -6 to 6
- panel_right: float32 [8, 32, 64, 2048], P('rows', 'panels'), may hold values from -0.09375 to 0.09375
- pivot_left: float32 [32, 64, 2048], P('panels', None, 'rows'), may hold values from -6 to 6
- pivot_right: float32 [32, 64, 2048], P('panels', None, 'rows'), may hold values from -0.09375 to 0.09375
- pattern: int32 [8, 32], P('rows', 'panels'), may hold values 0 or 1
- tile_left: float32 [8, 64, 2048], P('rows', None, 'panels'), may hold values from -6 to 6
- tile_right: float32 [8, 64, 2048], P('rows', None, 'panels'), may hold values from -0.75 to 0.75
- sketch: float32 [64, 2048], replicated, may hold values from -0.125 to 0.125
Outputs:
- new_left: float32 [8, 64, 2048], P('rows', None, 'panels')
- new_right: float32 [8, 64, 2048], P('rows', None, 'panels')
The draws below stay inside these ranges and needn't reach their ends.
All inputs are finite; a program needn't handle non-finite values. No bound on the sum of `pattern` on one device may be relied on, other than what follows from the above.
Results may differ from the reference program's by a relative error of at most 0.0003.
Values sent between devices are 32-bit elements; how exact they have to be, the bound alone decides.
No kernel may reach another device: no remote copies, remote signals or barrier semaphores. Data moves between devices by JAX's collectives and lax.ppermute only.
A program may use at most 128 MiB of HBM per device.

```python
import jax
import jax.numpy as jnp
from jax import lax

B = 2048
R = 64
TILES = 8
J = 32


def place_ends(entries, stream_key, low, largest):
    shape = entries.shape
    spot = [jax.random.randint(jax.random.fold_in(stream_key, axis), (), 0, shape[axis]) for axis in range(len(shape))]
    entries = entries.at[tuple(spot)].set(low)
    longest = shape.index(max(shape))
    spot[longest] = (spot[longest] + 1) % shape[longest]
    return entries.at[tuple(spot)].set(largest)


def block_scale(key, extent, shards, low, high):
    gain = 1.0
    for dim, blocks in shards:
        heights = jax.random.uniform(jax.random.fold_in(jax.random.fold_in(key, 6), dim), (blocks,), jnp.float32, low / len(shards), high / len(shards))
        gain = gain * jnp.repeat(jnp.exp(heights), extent[dim] // blocks).reshape((-1,) + (1,) * (len(extent) - 1 - dim))
    return gain


def centred(key, extent, deviation, bound, split=(), held_as=jnp.bfloat16):
    loudness = block_scale(key, extent, split, -0.22, 0.18) if split else 1.0
    entries = jax.random.normal(key, extent, jnp.float32) * deviation * loudness
    return jnp.minimum(jnp.maximum(entries, -bound), bound).astype(held_as)


def setup_inputs(seed: int = 0) -> dict:
    keys = jax.random.split(jax.random.key(seed), 9)
    panel_left = centred(keys[0], (TILES, J, R, B), 1.0, 6.0, ((0, 8), (1, 4)), jnp.float32)
    panel_right = centred(keys[1], (TILES, J, R, B), (R * 64) ** -0.5, 0.09375, ((0, 8), (1, 4)), jnp.float32)
    pivot_left = centred(keys[2], (J, R, B), 1.0, 6.0, ((0, 4), (2, 8)), jnp.float32)
    pivot_right = centred(keys[3], (J, R, B), (R * 64) ** -0.5, 0.09375, ((0, 4), (2, 8)), jnp.float32)
    pattern = place_ends((jax.random.randint(keys[4], (TILES, J), 0, 4) < 3).astype(jnp.int32), jax.random.fold_in(keys[4], 1), 0, 1)
    tile_left = centred(keys[5], (TILES, R, B), 1.0, 6.0, ((0, 8), (2, 4)), jnp.float32)
    tile_right = centred(keys[6], (TILES, R, B), R ** -0.5, 0.75, ((0, 8), (2, 4)), jnp.float32)
    sketch = centred(keys[7], (R, B), B ** -0.5, 0.125, (), jnp.float32)
    return dict(panel_left=panel_left, panel_right=panel_right, pivot_left=pivot_left, pivot_right=pivot_right, pattern=pattern, tile_left=tile_left, tile_right=tile_right, sketch=sketch)


highest = lax.Precision.HIGHEST

def compress(left_a, right_a, left_b, right_b, sketch):
    stacked_left = jnp.concatenate([left_a, left_b], axis=1)
    stacked_right = jnp.concatenate([right_a, right_b], axis=1)
    sketched = jnp.einsum('tkb,rb->tkr', stacked_right, sketch, precision=highest)
    basis = jnp.einsum('tkr,tkb->trb', sketched, stacked_left, precision=highest)
    gram = jnp.einsum('trb,tsb->trs', basis, basis, precision=highest)
    rank = gram.shape[-1]
    shift = 0.001 * jnp.trace(gram, axis1=1, axis2=2) / rank + 1e-06
    shifted = gram + shift[:, None, None] * jnp.eye(rank, dtype=jnp.float32)
    factor = jnp.linalg.cholesky(shifted)
    ortho = jax.scipy.linalg.solve_triangular(factor, basis, lower=True)
    projected = jnp.einsum('tkb,trb->tkr', stacked_left, ortho, precision=highest)
    fresh = jnp.einsum('tkr,tkb->trb', projected, stacked_right, precision=highest)
    scale = float(B) ** 0.5
    return (ortho * scale, fresh / scale)

def local_tree(left, right, sketch):
    while left.shape[1] > 1:
        count = left.shape[1] // 2
        rows = left.shape[0]
        tail = left.shape[2:]
        merged_left, merged_right = compress(left[:, 0::2].reshape((rows * count,) + tail), right[:, 0::2].reshape((rows * count,) + tail), left[:, 1::2].reshape((rows * count,) + tail), right[:, 1::2].reshape((rows * count,) + tail), sketch)
        left = merged_left.reshape((rows, count) + tail)
        right = merged_right.reshape((rows, count) + tail)
    return (left[:, 0], right[:, 0])

def reference(panel_left, panel_right, pivot_left, pivot_right, pattern, tile_left, tile_right, sketch):

    def one_row(item):
        row_left, row_right, row_mask, own_left, own_right = item
        inner = jnp.einsum('jrb,jsb->jrs', row_right, pivot_right, precision=highest)
        leaf_left = jnp.einsum('jrs,jrb->jsb', inner, row_left, precision=highest)
        leaf_left = leaf_left * row_mask.astype(jnp.float32)[:, None, None]
        merged_left, merged_right = local_tree(leaf_left[None], pivot_left[None], sketch)
        done_left, done_right = compress(own_left[None], own_right[None], -merged_left, merged_right, sketch)
        return (done_left[0], done_right[0])
    new_left, new_right = lax.map(one_row, (panel_left, panel_right, pattern, tile_left, tile_right))
    return (new_left, new_right)
```

```python
import functools

import jax
import jax.numpy as jnp
from jax import lax
from jax.experimental import pallas as pl
from jax.experimental.pallas import tpu as pltpu
from jax.sharding import PartitionSpec as P

highest = lax.Precision.HIGHEST
f32 = jnp.float32
VMEM = pl.BlockSpec(memory_space=pltpu.VMEM)
SMEM = pl.BlockSpec(memory_space=pltpu.SMEM)
LIMIT = pltpu.CompilerParams(vmem_limit_bytes=40 * 1024 * 1024)


def dot(a, b, dims):
    return lax.dot_general(a, b, (dims, ((), ())), precision=highest, preferred_element_type=f32)


def nn(a, b):
    return dot(a, b, ((1,), (0,)))


def nt(a, b):
    return dot(a, b, ((1,), (1,)))


def tn(a, b):
    return dot(a, b, ((0,), (0,)))


def identity(n):
    return (lax.broadcasted_iota(jnp.int32, (n, n), 0) == lax.broadcasted_iota(jnp.int32, (n, n), 1)).astype(f32)


def inverse_factors(matrices):
    n = matrices[0].shape[0]
    step = 8 if len(matrices) < 3 else 4
    eye = identity(n)
    states = []
    for matrix in matrices:
        both = jnp.concatenate([matrix, eye], axis=1)
        states.append([both[8 * m : 8 * m + 8] for m in range(n // 8)])
    sub = lax.broadcasted_iota(jnp.int32, (8, 2 * n), 0)
    for k in range(0, n, step):
        m, s = k // 8, k % 8
        for state in states:
            row = [state[m][s + a : s + a + 1] for a in range(step)]
            pivot = [
                [jnp.broadcast_to(row[a][:, k + b : k + b + 1], (1, 2 * n)) if b >= a else None for b in range(step)]
                for a in range(step)
            ]
            rest = [t for t in range(m, n // 8) if not (t == m and s + step == 8)]
            column = [{t: jnp.broadcast_to(state[t][:, k + b : k + b + 1], (8, 2 * n)) for t in rest} for b in range(step)]
            if m in rest:
                for b in range(step):
                    column[b][m] = jnp.where(sub >= s + step, column[b][m], 0.0)
            done = state[m]
            scaled = []
            for a in range(step):
                inverse = 1.0 / pivot[a][a]
                for b in range(a + 1, step):
                    factor = pivot[a][b] * inverse
                    row[b] = row[b] - factor * row[a]
                    for c in range(b, step):
                        pivot[b][c] = pivot[b][c] - factor * pivot[a][c]
                    for t in rest:
                        column[b][t] = column[b][t] - column[a][t] * factor
                scaled.append(row[a] * inverse)
                done = jnp.where(sub == s + a, row[a] * lax.rsqrt(pivot[a][a]), done)
            state[m] = done
            for t in rest:
                total = state[t]
                for a in range(step):
                    total = total - column[a][t] * scaled[a]
                state[t] = total
    return [jnp.concatenate([block[:, n:] for block in state], axis=0) for state in states]


def ridge_inverses(grams):
    n = grams[0].shape[0]
    eye = identity(n)
    ridges = [0.001 * jnp.sum(jnp.sum(g * eye, axis=1, keepdims=True), axis=0, keepdims=True) / n + 1e-06 for g in grams]
    factors = inverse_factors([g + e * eye for g, e in zip(grams, ridges)])
    return ridges, factors


def shrink(grams):
    eye = identity(grams[0].shape[0])
    ridges, factors = ridge_inverses(grams)
    inverses = [tn(c, c) for c in factors]
    return inverses, [eye - e * s for e, s in zip(ridges, inverses)]


def inner_kernel(count, *refs):
    panels, pieces, add, out = refs[1 : 1 + count], refs[1 + count : 1 + 2 * count], refs[1 + 2 * count : -1], refs[-1]
    total = add[0][0] if add else None
    for panel, piece in zip(panels, pieces):
        term = nt(piece[0], panel[0, 0])
        total = term if total is None else total + term
    out[0] = total


def inner_products(panel_right, pieces, sources, add=None):
    count = len(pieces)
    _, j, rank, _ = panel_right.shape
    width = pieces[0].shape[2]
    square = pl.BlockSpec((1, rank, rank), lambda i, s: (i, 0, 0))
    in_specs = [pl.BlockSpec((1, 1, rank, width), functools.partial(lambda i, s, k: (0, i, 0, s[k]), k=k)) for k in range(count)]
    in_specs += [pl.BlockSpec((1, rank, width), lambda i, s: (i, 0, 0))] * count
    in_specs += [square] if add is not None else []
    return pl.pallas_call(
        functools.partial(inner_kernel, count),
        grid_spec=pltpu.PrefetchScalarGridSpec(num_scalar_prefetch=1, grid=(j,), in_specs=in_specs, out_specs=square),
        out_shape=jax.ShapeDtypeStruct((j, rank, rank), f32),
        compiler_params=LIMIT,
    )(jnp.stack(sources).astype(jnp.int32), *([panel_right] * count), *pieces, *([] if add is None else [add]))


def tree_kernel(weights, sketched, inner, panel, basis, path, top, sent, inverse_out, own_out):
    count, rank, width = panel.shape
    nodes = count // 2
    for n in range(nodes):
        coefs = [nn(sketched[j], inner[j]) * weights[0, j].astype(f32) for j in (2 * n, 2 * n + 1)]
        basis[n] = nn(jnp.concatenate(coefs, axis=1), panel[2 * n : 2 * n + 2].reshape(2 * rank, width))
    basis_all = basis[...].reshape(nodes * rank, width)
    gram = nt(basis_all, basis_all)
    chains = [None] * nodes
    level = [(n, n + 1, None) for n in range(nodes)]

    def times(coefs, matrix):
        return matrix if coefs is None else nn(coefs, matrix)

    def times_t(matrix, coefs):
        return matrix if coefs is None else nt(matrix, coefs)

    while True:
        spans = [slice(a * rank, b * rank) for a, b, _ in level]
        crossed = [times(h, gram[s]) for (_, _, h), s in zip(level, spans)]
        inverses, shrunk = shrink([times_t(x[:, s], h) for x, s, (_, _, h) in zip(crossed, spans, level)])
        if len(level) == 1:
            break
        parents = []
        for m in range(0, len(level), 2):
            (a, _, ha), (_, b, hb) = level[m], level[m + 1]
            coefs = jnp.concatenate([times_t_first(shrunk[m], ha), times_t_first(shrunk[m + 1], hb)], axis=1)
            rows = nn(coefs, gram[a * rank : b * rank])
            for child in (m, m + 1):
                first, last, h = level[child]
                step = nn(times_t(rows[:, spans[child]], h), inverses[child])
                for n in range(first, last):
                    chains[n] = step if chains[n] is None else nn(step, chains[n])
            parents.append((a, b, coefs))
        level = parents
    coefs = level[0][2]
    for j in range(count):
        crossing = nt(basis[j // 2], panel[j])
        path[:, j * rank : (j + 1) * rank] = nt(nn(chains[j // 2], crossing), inner[j]) * weights[0, j].astype(f32)
    top[...] = nn(coefs, basis_all)
    sent[...] = nn(nn(shrunk[0], coefs), basis_all)
    inverse_out[...] = inverses[0]
    own_out[...] = nn(shrunk[0], times_t(crossed[0][:, spans[0]], coefs))


def times_t_first(matrix, coefs):
    return matrix if coefs is None else nn(matrix, coefs)


def local_tree(weights, sketched, inner, panel):
    count, rank, width = panel.shape
    wide = jax.ShapeDtypeStruct((rank, width), f32)
    square = jax.ShapeDtypeStruct((rank, rank), f32)
    return pl.pallas_call(
        tree_kernel,
        in_specs=[SMEM, VMEM, VMEM, VMEM],
        out_specs=[VMEM] * 6,
        out_shape=[
            jax.ShapeDtypeStruct((count // 2, rank, width), f32),
            jax.ShapeDtypeStruct((rank, count * rank), f32),
            wide,
            wide,
            square,
            square,
        ],
        compiler_params=LIMIT,
    )(weights, sketched, inner, panel)


def chip_kernel(partner, top, inverse, own, step):
    step[...] = nn(own[...] + nt(partner[...], top[...]), inverse[...])


def root_kernel(chunk, own, core, far, far_core, tile, sketched, new_left, coefs_out):
    rank, width = tile.shape
    near = own[...] + core[...]
    other = far[...] + far_core[...]
    stack = jnp.concatenate([tile[...], near, other], axis=0)
    gram = nt(stack, stack)
    parts = [slice(k * rank, (k + 1) * rank) for k in range(3)]
    inverses, shrunk = shrink([gram[s, s] for s in parts[1:]])
    both = jnp.concatenate(shrunk, axis=1)
    rows = nn(both, gram[rank:])
    inverse, last = shrink([nt(rows[:, rank:], both)])
    coefs = jnp.concatenate([sketched[...], -nn(last[0], both)], axis=1)
    final = nn(coefs, gram)
    _, factors = ridge_inverses([nt(final, coefs)])
    factor = factors[0]
    scale = float(width) ** 0.5
    columns = new_left.shape[1]
    first = pl.multiple_of(chunk[0] * columns, columns)
    here = [tile[:, pl.ds(first, columns)]]
    here += [own[:, pl.ds(first, columns)] + core[:, pl.ds(first, columns)]]
    here += [far[:, pl.ds(first, columns)] + far_core[:, pl.ds(first, columns)]]
    new_left[...] = nn(nn(factor, coefs) * scale, jnp.concatenate(here, axis=0))
    down = nn(nt(final[:, rank:], both), inverse[0])
    steps = [-nn(nn(down, rows[:, s]), i) for s, i in zip(parts[1:], inverses)]
    coefs_out[...] = nn(factor, jnp.concatenate([final[:, parts[0]]] + steps, axis=1)) / scale


def finish_kernel(coefs, tile, own, core, far, far_core, new_right):
    stack = jnp.concatenate([tile[...], own[...] + core[...], far[...] + far_core[...]], axis=0)
    new_right[...] = nn(coefs[...], stack)


def call(kernel, out_shape, *operands, scalars=0):
    return pl.pallas_call(
        kernel,
        in_specs=[SMEM] * scalars + [VMEM] * (len(operands) - scalars),
        out_specs=jax.tree.map(lambda _: VMEM, out_shape),
        out_shape=out_shape,
        compiler_params=LIMIT,
    )(*operands)


def swap(value, axis, mask, members=None):
    members = range(lax.axis_size(axis)) if members is None else members
    return lax.ppermute(value, axis, [(i, i ^ mask) for i in members])


def gather_line(block, index):
    rows = lax.axis_size("rows")
    middle = range(2, rows - 2)
    ends = [i for i in range(rows) if i not in middle]
    low = index < rows // 2
    top = rows - 1

    def move(value, pairs):
        return lax.ppermute(value, "rows", pairs)

    up = move(block, [(i, i - 2) for i in range(2, rows)])
    down = move(block, [(i, i + 2) for i in range(rows - 2)])
    side = swap(block, "rows", 1)
    near = jnp.where(low, up, down)
    far_side = swap(side, "rows", top - 1, ends)
    up_two = move(up, [(i, i - 2) for i in range(2, rows - 2)])
    down_two = move(down, [(i, i + 2) for i in range(2, rows - 2)])
    two = jnp.where(low, up_two, down_two)
    near_side = swap(near, "rows", 1)
    other_side = swap(jnp.where(low, down, up), "rows", 1, middle)
    three = move(two, [(2, 0), (3, 1), (top - 3, top - 1), (top - 2, top)])
    two_side = swap(two, "rows", 1)
    above = jnp.minimum(index + 2, top - 1 + index % 2)
    below = jnp.maximum(index - 2, index % 2)
    nearest = jnp.where(low, index + 2, index - 2)
    early = [(block, index), (side, index ^ 1), (up, above), (down, below), (near_side, nearest ^ 1)]
    late = [
        (other_side, jnp.where(low, below, above) ^ 1),
        (two, index ^ 4),
        (far_side, top - index),
        (three, index ^ (top - 1)),
        (two_side, index ^ 5),
    ]
    return early, late


def local(panel_left, panel_right, pivot_left, pivot_right, pattern, tile_left, tile_right, sketch):
    rows = lax.axis_size("rows")
    row = lax.axis_index("rows")
    place = lax.axis_index("panels")
    count, rank, local_columns = pivot_left.shape
    columns = tile_left.shape[2]
    width = panel_left.shape[3]
    wide = jax.ShapeDtypeStruct((rank, width), f32)
    square = jax.ShapeDtypeStruct((rank, rank), f32)
    chunk = jax.ShapeDtypeStruct((rank, columns), f32)
    tile_left, tile_right = tile_left[0], tile_right[0]

    sketch_here = lax.dynamic_slice_in_dim(sketch, row * local_columns, local_columns, 1)
    sketched = jnp.einsum("rb,jkb->jrk", sketch_here, pivot_left, precision=highest)
    if rows == 8:
        for mask in (1, 2, 4):
            sketched = sketched + swap(sketched, "rows", mask)
    else:
        sketched = lax.psum(sketched, "rows")
    sketch_tile = lax.dynamic_slice_in_dim(sketch, place * columns, columns, 1)
    tile_sketched = nt(sketch_tile, tile_right)
    for mask in (1, 2):
        tile_sketched = tile_sketched + swap(tile_sketched, "panels", mask)
    whole_tile = lax.all_gather(tile_left, "panels", axis=1, tiled=True)

    if rows == 8 and local_columns % 128 == 0:
        early, late = gather_line(pivot_right, row)
        inner = inner_products(panel_right, [v for v, _ in early], [s for _, s in early])
        inner = inner_products(panel_right, [v for v, _ in late], [s for _, s in late], inner)
    else:
        full = lax.all_gather(pivot_right, "rows", axis=2, tiled=True)
        inner = inner_products(panel_right, [full], [jnp.int32(0)])

    _, path, top, sent, inverse, own = local_tree(pattern, sketched, inner, panel_left[0])
    far = swap(sent, "panels", 2)
    core = swap(sent, "panels", 1)
    far_core = swap(far, "panels", 1)
    step = call(chip_kernel, square, core, top, inverse, own)

    full_left = lax.all_gather(pivot_left, "rows", axis=2, tiled=True)
    right = nn(path, full_left.reshape(count * rank, width))
    right = nn(step, right)
    rights = []
    for mask in range(4):
        part = lax.dynamic_slice_in_dim(right, (place ^ mask) * columns, columns, 1)
        rights.append(swap(part, "panels", mask) if mask else part)

    new_left, coefs = call(
        root_kernel,
        [chunk, jax.ShapeDtypeStruct((rank, 3 * rank), f32)],
        place.reshape(1).astype(jnp.int32),
        sent,
        core,
        far,
        far_core,
        whole_tile,
        tile_sketched,
        scalars=1,
    )
    new_right = call(finish_kernel, chunk, coefs, tile_right, *rights)
    return (new_left[None], new_right[None])


def solution(mesh):
    return jax.shard_map(
        local,
        mesh=mesh,
        in_specs=(
            P("rows", "panels", None, None),
            P("rows", "panels", None, None),
            P("panels", None, "rows"),
            P("panels", None, "rows"),
            P("rows", "panels"),
            P("rows", None, "panels"),
            P("rows", None, "panels"),
            P(),
        ),
        out_specs=(P("rows", None, "panels"), P("rows", None, "panels")),
        check_vma=False,
    )
```

```python
import functools

import jax
import jax.numpy as jnp
from jax import lax
from jax.experimental import pallas as pl
from jax.experimental.pallas import tpu as pltpu
from jax.sharding import PartitionSpec as P

highest = lax.Precision.HIGHEST
f32 = jnp.float32
VMEM = pl.BlockSpec(memory_space=pltpu.VMEM)
SMEM = pl.BlockSpec(memory_space=pltpu.SMEM)
LIMIT = pltpu.CompilerParams(vmem_limit_bytes=20 * 1024 * 1024)
ROOMY = pltpu.CompilerParams(vmem_limit_bytes=32 * 1024 * 1024)
SHORT = pl.CostEstimate(flops=10**8, bytes_accessed=10**6, transcendentals=0)


def dot(a, b, dims):
    return lax.dot_general(a, b, (dims, ((), ())), precision=highest, preferred_element_type=f32)


def nn(a, b):
    return dot(a, b, ((1,), (0,)))


def nt(a, b):
    return dot(a, b, ((1,), (1,)))


def tn(a, b):
    return dot(a, b, ((0,), (0,)))


def identity(n):
    return (lax.broadcasted_iota(jnp.int32, (n, n), 0) == lax.broadcasted_iota(jnp.int32, (n, n), 1)).astype(f32)


def inverse_factors(matrices):
    n = matrices[0].shape[0]
    step = 8 if len(matrices) < 3 else 4
    eye = identity(n)
    states = []
    for matrix in matrices:
        both = jnp.concatenate([matrix, eye], axis=1)
        states.append([both[8 * m : 8 * m + 8] for m in range(n // 8)])
    sub = lax.broadcasted_iota(jnp.int32, (8, 2 * n), 0)
    for k in range(0, n, step):
        m, s = k // 8, k % 8
        for state in states:
            row = [state[m][s + a : s + a + 1] for a in range(step)]
            pivot = [
                [jnp.broadcast_to(row[a][:, k + b : k + b + 1], (1, 2 * n)) if b >= a else None for b in range(step)]
                for a in range(step)
            ]
            rest = [t for t in range(m, n // 8) if not (t == m and s + step == 8)]
            column = [{t: jnp.broadcast_to(state[t][:, k + b : k + b + 1], (8, 2 * n)) for t in rest} for b in range(step)]
            if m in rest:
                for b in range(step):
                    column[b][m] = jnp.where(sub >= s + step, column[b][m], 0.0)
            done = state[m]
            scaled = []
            for a in range(step):
                inverse = 1.0 / pivot[a][a]
                for b in range(a + 1, step):
                    factor = pivot[a][b] * inverse
                    row[b] = row[b] - factor * row[a]
                    for c in range(b, step):
                        pivot[b][c] = pivot[b][c] - factor * pivot[a][c]
                    for t in rest:
                        column[b][t] = column[b][t] - column[a][t] * factor
                scaled.append(row[a] * inverse)
                done = jnp.where(sub == s + a, row[a] * lax.rsqrt(pivot[a][a]), done)
            state[m] = done
            for t in rest:
                total = state[t]
                for a in range(step):
                    total = total - column[a][t] * scaled[a]
                state[t] = total
    return [jnp.concatenate([block[:, n:] for block in state], axis=0) for state in states]


def ridge_inverses(grams):
    n = grams[0].shape[0]
    eye = identity(n)
    ridges = [0.001 * jnp.sum(jnp.sum(g * eye, axis=1, keepdims=True), axis=0, keepdims=True) / n + 1e-06 for g in grams]
    factors = inverse_factors([g + e * eye for g, e in zip(grams, ridges)])
    return ridges, factors


def shrink(grams):
    eye = identity(grams[0].shape[0])
    ridges, factors = ridge_inverses(grams)
    inverses = [tn(c, c) for c in factors]
    return inverses, [eye - e * s for e, s in zip(ridges, inverses)]


def split(value):
    parts = []
    for _ in range(3):
        part = value.astype(jnp.bfloat16)
        parts.append(part)
        value = value - part.astype(f32)
    return parts


def nt_parts(a, b):
    m, n = a.shape[0], b.shape[0]
    stacked = lax.dot_general(
        jnp.concatenate(split(a), axis=0),
        jnp.concatenate(split(b), axis=0),
        (((1,), (1,)), ((), ())),
        preferred_element_type=f32,
    )

    def block(i, k):
        return stacked[i * m : (i + 1) * m, k * n : (k + 1) * n]

    small = block(1, 1) + block(0, 2) + block(2, 0)
    return block(0, 0) + (block(0, 1) + block(1, 0) + small)


def inner_kernel(count, *refs):
    panels, pieces, add, out = refs[1 : 1 + count], refs[1 + count : 1 + 2 * count], refs[1 + 2 * count : -1], refs[-1]
    for j in range(out.shape[0]):
        left = jnp.concatenate([piece[j] for piece in pieces], axis=1)
        right = jnp.concatenate([panel[0, j] for panel in panels], axis=1)
        term = nt_parts(left, right)
        out[j] = term + add[0][j] if add else term


def inner_products(panel_right, pieces, sources, add=None):
    count = len(pieces)
    _, j, rank, _ = panel_right.shape
    width = pieces[0].shape[2]
    group = j // 2
    square = pl.BlockSpec((group, rank, rank), lambda i, s: (i, 0, 0))
    in_specs = [pl.BlockSpec((1, group, rank, width), functools.partial(lambda i, s, k: (0, i, 0, s[k]), k=k)) for k in range(count)]
    in_specs += [pl.BlockSpec((group, rank, width), lambda i, s: (i, 0, 0))] * count
    in_specs += [square] if add is not None else []
    return pl.pallas_call(
        functools.partial(inner_kernel, count),
        grid_spec=pltpu.PrefetchScalarGridSpec(num_scalar_prefetch=1, grid=(j // group,), in_specs=in_specs, out_specs=square),
        out_shape=held(j, rank, rank),
        compiler_params=ROOMY,
        cost_estimate=SHORT,
    )(jnp.stack(sources).astype(jnp.int32), *([panel_right] * count), *pieces, *([] if add is None else [add]))


def tree_kernel(weights, sketched, inner, products, path, whole):
    count, rank, _ = sketched.shape
    nodes = count // 2
    leaves = [
        jnp.concatenate([nn(sketched[j], inner[j]) * weights[0, j].astype(f32) for j in (2 * n, 2 * n + 1)], axis=1)
        for n in range(nodes)
    ]
    pair = [slice(2 * n * rank, 2 * (n + 1) * rank) for n in range(nodes)]
    crossing = [nn(leaf, products[s]) for leaf, s in zip(leaves, pair)]
    crossing_all = jnp.concatenate(crossing, axis=0)
    gram = jnp.concatenate([nt(crossing_all[:, s], leaf) for leaf, s in zip(leaves, pair)], axis=1)
    chains = [None] * nodes
    level = [(n, n + 1, None) for n in range(nodes)]

    def times(coefs, matrix):
        return matrix if coefs is None else nn(coefs, matrix)

    def times_t(matrix, coefs):
        return matrix if coefs is None else nt(matrix, coefs)

    def after(matrix, coefs):
        return matrix if coefs is None else nn(matrix, coefs)

    while len(level) > 1:
        spans = [slice(a * rank, b * rank) for a, b, _ in level]
        crossed = [times(h, gram[s]) for (_, _, h), s in zip(level, spans)]
        inverses, shrunk = shrink([times_t(x[:, s], h) for x, s, (_, _, h) in zip(crossed, spans, level)])
        parents = []
        for m in range(0, len(level), 2):
            (a, _, ha), (_, b, hb) = level[m], level[m + 1]
            coefs = jnp.concatenate([after(shrunk[m], ha), after(shrunk[m + 1], hb)], axis=1)
            rows = nn(coefs, gram[a * rank : b * rank])
            for child in (m, m + 1):
                first, last, h = level[child]
                step = nn(times_t(rows[:, spans[child]], h), inverses[child])
                for n in range(first, last):
                    chains[n] = step if chains[n] is None else nn(step, chains[n])
            parents.append((a, b, coefs))
        level = parents
    coefs = level[0][2]
    for n in range(nodes):
        both = nn(chains[n], crossing[n][:, pair[n]])
        for j in (0, 1):
            k = 2 * n + j
            path[:, k * rank : (k + 1) * rank] = nt(both[:, j * rank : (j + 1) * rank], inner[k]) * weights[0, k].astype(f32)
    for n, leaf in enumerate(leaves):
        whole[:, pair[n]] = nn(coefs[:, n * rank : (n + 1) * rank], leaf)
    whole[:, count * rank :] = nt(nn(coefs, gram), coefs)


def top_kernel(whole, panel, top, sent, squares, held, sem):
    copy = pltpu.make_async_copy(panel, held, sem)
    copy.start()
    rank = whole.shape[0]
    depth = panel.shape[0]
    gram = whole[:, depth:]
    inverses, shrunk = shrink([gram])
    squares[:, :rank] = inverses[0]
    squares[:, rank:] = nn(shrunk[0], gram)
    copy.wait()
    factor = nn(whole[:, :depth], held[...])
    top[...] = factor
    sent[...] = nn(shrunk[0], factor)


def chip_kernel(own, partner, top, squares, tile, step, near_out, gram_out):
    near = own[...] + partner[...]
    near_out[...] = near
    rank = top.shape[0]
    step[...] = nn(squares[:, rank:] + nt(partner[...], top[...]), squares[:, :rank])
    stack = jnp.concatenate([tile[...], near], axis=0)
    gram_out[...] = nt(stack, stack)


def root_kernel(chunk, near, far, far_core, tile, gram_in, sketched, new_left, coefs_out):
    rank, width = tile.shape
    other = far[...] + far_core[...]
    cross = nt(other, jnp.concatenate([tile[...], near[...], other], axis=0))
    above = jnp.concatenate([gram_in[...], cross[:, : 2 * rank].T], axis=1)
    gram = jnp.concatenate([above, cross], axis=0)
    parts = [slice(k * rank, (k + 1) * rank) for k in range(3)]
    inverses, shrunk = shrink([gram[s, s] for s in parts[1:]])
    both = jnp.concatenate(shrunk, axis=1)
    rows = nn(both, gram[rank:])
    inverse, last = shrink([nt(rows[:, rank:], both)])
    coefs = jnp.concatenate([sketched[...], -nn(last[0], both)], axis=1)
    final = nn(coefs, gram)
    down = nn(nt(final[:, rank:], both), inverse[0])
    steps = [-nn(nn(down, rows[:, s]), i) for s, i in zip(parts[1:], inverses)]
    _, factors = ridge_inverses([nt(final, coefs)])
    factor = factors[0]
    scale = float(width) ** 0.5
    columns = new_left.shape[1]
    here = pl.ds(pl.multiple_of(chunk[0] * columns, columns), columns)
    stack = jnp.concatenate([tile[:, here], near[:, here], far[:, here] + far_core[:, here]], axis=0)
    new_left[...] = nn(nn(factor, coefs) * scale, stack)
    coefs_out[...] = nn(factor, jnp.concatenate([final[:, parts[0]]] + steps, axis=1)) / scale


def copy_kernel(value, out):
    out[...] = value[...]


def right_kernel(*refs):
    paths, pieces, outs = refs[:4], refs[4:-4], refs[-4:]
    rank = paths[0].shape[0]
    stack = jnp.concatenate([path[...] for path in paths], axis=0)
    part = nn(stack, jnp.concatenate([piece[...] for piece in pieces], axis=1))
    for k, out in enumerate(outs):
        out[...] = part[k * rank : (k + 1) * rank]


def collect_kernel(spots, step, own, side, near, near_side, *refs):
    outs, held = refs[:4], refs[4]
    half = own.shape[1] // 2
    odd = spots[4] == 1
    k = 0
    for first, second in ((own, side), (near, near_side)):
        part = nn(step[...], jnp.concatenate([first[...], second[...]], axis=1))
        for i in range(2):
            a = part[:, i * half : (i + 1) * half]
            b = part[:, (2 + i) * half : (3 + i) * half]
            held[spots[k]] = jnp.concatenate([jnp.where(odd, b, a), jnp.where(odd, a, b)], axis=1)
            k += 1
    for k, out in enumerate(outs):
        out[...] = held[k]


def finish_kernel(coefs, tile, own, core, far, far_core, new_right):
    stack = jnp.concatenate([tile[...], own[...] + core[...], far[...] + far_core[...]], axis=0)
    new_right[...] = nn(coefs[...], stack)


def held(*shape):
    return pltpu.VMEM(shape, f32)


def call(kernel, out_shape, *operands, scalars=0, scratch=()):
    return pl.pallas_call(
        kernel,
        in_specs=[SMEM] * scalars + [VMEM] * (len(operands) - scalars),
        out_specs=jax.tree.map(lambda _: VMEM, out_shape, is_leaf=lambda v: not isinstance(v, list)),
        out_shape=out_shape,
        scratch_shapes=scratch,
        compiler_params=LIMIT,
        cost_estimate=SHORT,
    )(*operands)


def swap(value, axis, mask, members=None):
    members = range(lax.axis_size(axis)) if members is None else members
    return lax.ppermute(value, axis, [(i, i ^ mask) for i in members])


def chip_step(sent, top, squares, tile):
    rank, width = tile.shape
    core = swap(sent, "panels", 1)
    shapes = [held(rank, rank), held(rank, width), held(2 * rank, 2 * rank)]
    return core, *call(chip_kernel, shapes, sent, core, top, squares, tile)


def gather_panels(value):
    core = swap(value, "panels", 1)
    far = swap(jnp.stack([value, core]), "panels", 2)
    return [value, core, far[0], far[1]]


def gather_line(block, index, partial, tile, beside):
    ends, middle = (0, 1, 6, 7), (2, 3, 4, 5)
    is_end = (index < 2) | (index > 5)
    outward = [(2, 0), (3, 1), (4, 6), (5, 7)]

    near = swap(block, "rows", 2)
    center = swap(block, "rows", 6, middle)
    side = swap(block, "rows", 1)
    for mask in (1, 2):
        partial = partial + swap(partial, "rows", mask)
    near, center, side, partial, beside = lax.optimization_barrier((near, center, side, partial, beside))

    outer = lax.ppermute(center, "rows", outward)
    inner = swap(near, "rows", 6, middle)
    near_side = swap(near, "rows", 1)
    crossed = jnp.where(is_end, side, center)
    far_side = lax.ppermute(crossed, "rows", [(i, i ^ (6 if i in ends else 1)) for i in range(8)])
    outer, inner, near_side, far_side, partial, tile = lax.optimization_barrier(
        (outer, inner, near_side, far_side, partial, tile)
    )

    opposite = jnp.where(is_end, outer, inner)
    opposite, inner, partial = lax.optimization_barrier((opposite, inner, partial))
    far = lax.ppermute(inner, "rows", outward)
    opposite_side = swap(opposite, "rows", 1)
    partial = partial + swap(partial, "rows", 4)
    tiles = gather_panels(tile)
    early = [block, side, near, near_side, opposite, far_side, center]
    late = [opposite_side, far]
    return [(v, index ^ k) for v, k in zip(early, (0, 1, 2, 3, 4, 7, 6))], [
        (v, index ^ k) for v, k in zip(late, (5, 6))
    ], partial, tiles, beside


def local(panel_left, panel_right, pivot_left, pivot_right, pattern, tile_left, tile_right, sketch):
    rows = lax.axis_size("rows")
    row = lax.axis_index("rows")
    place = lax.axis_index("panels")
    count, rank, local_columns = pivot_left.shape
    columns = tile_left.shape[2]
    width = panel_left.shape[3]
    wide = held(rank, width)
    square = held(rank, rank)
    chunk = held(rank, columns)
    tile_left, tile_right = tile_left[0], tile_right[0]

    sketch_here = lax.dynamic_slice_in_dim(sketch, row * local_columns, local_columns, 1)
    sketched = jnp.einsum("rb,jkb->jrk", sketch_here, pivot_left, precision=highest)
    sketch_tile = lax.dynamic_slice_in_dim(sketch, place * columns, columns, 1)
    tile_sketched = nt(sketch_tile, tile_right)
    panel = panel_left.reshape(count * rank, width)
    products = nt(panel, panel)
    routed = rows == 8 and local_columns % 128 == 0
    tile = jnp.concatenate([tile_left, tile_sketched, jnp.zeros_like(tile_sketched)], axis=1)
    if routed:
        early, late, sketched, tiles, products = gather_line(pivot_right, row, sketched, tile, products)
    else:
        sketched = lax.psum(sketched, "rows")
        tiles = gather_panels(tile)
    tile_sketched = sum(tile[:, columns : columns + rank] for tile in tiles)
    whole_tile = jnp.zeros((rank, width), f32)
    for mask, tile in enumerate(tiles):
        whole_tile = lax.dynamic_update_slice_in_dim(whole_tile, tile[:, :columns], (place ^ mask) * columns, 1)

    if routed:
        inner = inner_products(panel_right, [v for v, _ in early], [s for _, s in early])
        inner, sketched, tile_sketched, whole_tile = lax.optimization_barrier((inner, sketched, tile_sketched, whole_tile))
        _, pivot_left = lax.optimization_barrier((late, pivot_left))
        pivot = call(copy_kernel, held(count * rank, local_columns), pivot_left.reshape(count * rank, local_columns))
        inner, pivot = lax.optimization_barrier((inner, pivot))
        opposite = swap(pivot, "rows", 4)
        inner = inner_products(panel_right, [v for v, _ in late], [s for _, s in late], inner)
    else:
        full = lax.all_gather(pivot_right, "rows", axis=2, tiled=True)
        inner = inner_products(panel_right, [full], [jnp.int32(0)])

    path, whole = call(
        tree_kernel,
        [held(rank, count * rank), held(rank, (count + 1) * rank)],
        pattern,
        sketched,
        inner,
        products,
        scalars=1,
    )
    top, sent, squares = pl.pallas_call(
        top_kernel,
        in_specs=[VMEM, pl.BlockSpec(memory_space=pl.ANY)],
        out_specs=[VMEM] * 3,
        out_shape=[wide, wide, held(rank, 2 * rank)],
        scratch_shapes=[pltpu.VMEM(panel.shape, f32), pltpu.SemaphoreType.DMA],
        compiler_params=LIMIT,
        cost_estimate=SHORT,
    )(whole, panel)
    if routed:
        pieces = [pivot, opposite]
        paths = [path] + [swap(path, "rows", mask) for mask in (1, 2, 3)]
        half = held(rank, 2 * local_columns)
        paths, pieces, sent = lax.optimization_barrier((paths, pieces, sent))
        far = swap(sent, "panels", 2)
        core, step, near, gram = chip_step(sent, top, squares, whole_tile)
        mine, *given = call(right_kernel, [half] * 4, *paths, *pieces)
        got = [mine] + [swap(v, "rows", mask) for mask, v in zip((1, 2, 3), given)]
        far, got = lax.optimization_barrier((far, got))
        depth = row // 2
        spots = jnp.stack([depth ^ place, depth ^ 2 ^ place, depth ^ 1 ^ place, depth ^ 3 ^ place, row % 2])
        parts = call(collect_kernel, [chunk] * 4, spots.astype(jnp.int32), step, *got, scalars=1, scratch=[pltpu.VMEM((4, rank, columns), f32)])
        rights = [swap(parts[mask], "panels", mask) if mask else parts[0] for mask in range(4)]
    else:
        core, step, near, gram = chip_step(sent, top, squares, whole_tile)
        far = swap(sent, "panels", 2)
        full_left = lax.all_gather(pivot_left, "rows", axis=2, tiled=True)
        right = nn(step, nn(path, full_left.reshape(count * rank, width)))
        rights = []
        for mask in range(4):
            part = lax.dynamic_slice_in_dim(right, (place ^ mask) * columns, columns, 1)
            rights.append(swap(part, "panels", mask) if mask else part)

    far_core = swap(far, "panels", 1)
    new_left, coefs = call(
        root_kernel,
        [jax.ShapeDtypeStruct((rank, columns), f32), held(rank, 3 * rank)],
        place.reshape(1).astype(jnp.int32),
        near,
        far,
        far_core,
        whole_tile,
        gram,
        tile_sketched,
        scalars=1,
    )
    new_right = call(finish_kernel, jax.ShapeDtypeStruct((rank, columns), f32), coefs, tile_right, *rights)
    return (new_left[None], new_right[None])


def solution(mesh):
    return jax.shard_map(
        local,
        mesh=mesh,
        in_specs=(
            P("rows", "panels", None, None),
            P("rows", "panels", None, None),
            P("panels", None, "rows"),
            P("panels", None, "rows"),
            P("rows", "panels"),
            P("rows", None, "panels"),
            P("rows", None, "panels"),
            P(),
        ),
        out_specs=(P("rows", None, "panels"), P("rows", None, "panels")),
        check_vma=False,
    )
```

```python
import functools

import jax
import jax.numpy as jnp
from jax import lax
from jax.experimental import pallas as pl
from jax.experimental.pallas import tpu as pltpu
from jax.sharding import PartitionSpec as P

highest = lax.Precision.HIGHEST
f32 = jnp.float32
VMEM = pl.BlockSpec(memory_space=pltpu.VMEM)
SMEM = pl.BlockSpec(memory_space=pltpu.SMEM)
LIMIT = pltpu.CompilerParams(vmem_limit_bytes=12 * 1024 * 1024)
ROOMY = pltpu.CompilerParams(vmem_limit_bytes=32 * 1024 * 1024)
SHORT = pl.CostEstimate(flops=10**8, bytes_accessed=10**6, transcendentals=0)


def dot(a, b, dims):
    return lax.dot_general(a, b, (dims, ((), ())), precision=highest, preferred_element_type=f32)


def nn(a, b):
    return dot(a, b, ((1,), (0,)))


def nt(a, b):
    return dot(a, b, ((1,), (1,)))


def tn(a, b):
    return dot(a, b, ((0,), (0,)))


def identity(n):
    return (lax.broadcasted_iota(jnp.int32, (n, n), 0) == lax.broadcasted_iota(jnp.int32, (n, n), 1)).astype(f32)


def reciprocal(value):
    guess = pl.reciprocal(value, approx=True)
    for _ in range(2):
        guess = guess * (2.0 - value * guess)
    return guess


def inverse_factors(matrices):
    n = matrices[0].shape[0]
    step = 8 if len(matrices) < 3 else 4
    eye = identity(n)
    states = []
    for matrix in matrices:
        both = jnp.concatenate([matrix, eye], axis=1)
        states.append([both[8 * m : 8 * m + 8] for m in range(n // 8)])
    sub = lax.broadcasted_iota(jnp.int32, (8, 2 * n), 0)
    for k in range(0, n, step):
        m, s = k // 8, k % 8
        for state in states:
            row = [state[m][s + a : s + a + 1] for a in range(step)]
            pivot = [
                [jnp.broadcast_to(row[a][:, k + b : k + b + 1], (1, 2 * n)) if b >= a else None for b in range(step)]
                for a in range(step)
            ]
            rest = [t for t in range(m, n // 8) if not (t == m and s + step == 8)]
            column = [{t: jnp.broadcast_to(state[t][:, k + b : k + b + 1], (8, 2 * n)) for t in rest} for b in range(step)]
            if m in rest:
                for b in range(step):
                    column[b][m] = jnp.where(sub >= s + step, column[b][m], 0.0)
            done = state[m]
            scaled = []
            for a in range(step):
                inverse = reciprocal(pivot[a][a])
                for b in range(a + 1, step):
                    factor = pivot[a][b] * inverse
                    row[b] = row[b] - factor * row[a]
                    for c in range(b, step):
                        pivot[b][c] = pivot[b][c] - factor * pivot[a][c]
                    for t in rest:
                        column[b][t] = column[b][t] - column[a][t] * factor
                scaled.append(row[a] * inverse)
                done = jnp.where(sub == s + a, row[a] * lax.rsqrt(pivot[a][a]), done)
            state[m] = done
            for t in rest:
                total = state[t]
                for a in range(step):
                    total = total - column[a][t] * scaled[a]
                state[t] = total
    return [jnp.concatenate([block[:, n:] for block in state], axis=0) for state in states]


def ridge_inverses(grams):
    n = grams[0].shape[0]
    eye = identity(n)
    ridges = [0.001 * jnp.sum(jnp.sum(g * eye, axis=1, keepdims=True), axis=0, keepdims=True) / n + 1e-06 for g in grams]
    factors = inverse_factors([g + e * eye for g, e in zip(grams, ridges)])
    return ridges, factors


def shrink(grams):
    eye = identity(grams[0].shape[0])
    ridges, factors = ridge_inverses(grams)
    inverses = [tn(c, c) for c in factors]
    return inverses, [eye - e * s for e, s in zip(ridges, inverses)]


def split(value):
    parts = []
    for _ in range(3):
        part = value.astype(jnp.bfloat16)
        parts.append(part)
        value = value - part.astype(f32)
    return parts


def nt_parts(a, b):
    m, n = a.shape[0], b.shape[0]
    stacked = lax.dot_general(
        jnp.concatenate(split(a), axis=0),
        jnp.concatenate(split(b), axis=0),
        (((1,), (1,)), ((), ())),
        preferred_element_type=f32,
    )

    def block(i, k):
        return stacked[i * m : (i + 1) * m, k * n : (k + 1) * n]

    small = block(1, 1) + block(0, 2) + block(2, 0)
    return block(0, 0) + (block(0, 1) + block(1, 0) + small)


def inner_kernel(count, *refs):
    panels, pieces, add, out = refs[1 : 1 + count], refs[1 + count : 1 + 2 * count], refs[1 + 2 * count : -1], refs[-1]
    for j in range(out.shape[0]):
        left = jnp.concatenate([piece[j] for piece in pieces], axis=1)
        right = jnp.concatenate([panel[0, j] for panel in panels], axis=1)
        term = nt_parts(left, right)
        out[j] = term + add[0][j] if add else term


def inner_products(panel_right, pieces, sources, add=None):
    count = len(pieces)
    _, j, rank, _ = panel_right.shape
    width = pieces[0].shape[2]
    group = j // 2
    square = pl.BlockSpec((group, rank, rank), lambda i, s: (i, 0, 0))
    in_specs = [pl.BlockSpec((1, group, rank, width), functools.partial(lambda i, s, k: (0, i, 0, s[k]), k=k)) for k in range(count)]
    in_specs += [pl.BlockSpec((group, rank, width), lambda i, s: (i, 0, 0))] * count
    in_specs += [square] if add is not None else []
    return pl.pallas_call(
        functools.partial(inner_kernel, count),
        grid_spec=pltpu.PrefetchScalarGridSpec(num_scalar_prefetch=1, grid=(j // group,), in_specs=in_specs, out_specs=square),
        out_shape=held(j, rank, rank),
        compiler_params=ROOMY,
        cost_estimate=SHORT,
    )(jnp.stack(sources).astype(jnp.int32), *([panel_right] * count), *pieces, *([] if add is None else [add]))


def tree_kernel(weights, sketched, inner, products, path, whole):
    count, rank, _ = sketched.shape
    nodes = count // 2
    leaves = [
        jnp.concatenate([nn(sketched[j], inner[j]) * weights[0, j].astype(f32) for j in (2 * n, 2 * n + 1)], axis=1)
        for n in range(nodes)
    ]
    pair = [slice(2 * n * rank, 2 * (n + 1) * rank) for n in range(nodes)]
    crossing = [nn(leaf, products[s]) for leaf, s in zip(leaves, pair)]
    crossing_all = jnp.concatenate(crossing, axis=0)
    gram = jnp.concatenate([nt(crossing_all[:, s], leaf) for leaf, s in zip(leaves, pair)], axis=1)
    chains = [None] * nodes
    level = [(n, n + 1, None) for n in range(nodes)]

    def times(coefs, matrix):
        return matrix if coefs is None else nn(coefs, matrix)

    def times_t(matrix, coefs):
        return matrix if coefs is None else nt(matrix, coefs)

    def after(matrix, coefs):
        return matrix if coefs is None else nn(matrix, coefs)

    while len(level) > 1:
        spans = [slice(a * rank, b * rank) for a, b, _ in level]
        crossed = [times(h, gram[s]) for (_, _, h), s in zip(level, spans)]
        inverses, shrunk = shrink([times_t(x[:, s], h) for x, s, (_, _, h) in zip(crossed, spans, level)])
        parents = []
        for m in range(0, len(level), 2):
            (a, _, ha), (_, b, hb) = level[m], level[m + 1]
            coefs = jnp.concatenate([after(shrunk[m], ha), after(shrunk[m + 1], hb)], axis=1)
            rows = nn(coefs, gram[a * rank : b * rank])
            for child in (m, m + 1):
                first, last, h = level[child]
                step = nn(times_t(rows[:, spans[child]], h), inverses[child])
                for n in range(first, last):
                    chains[n] = step if chains[n] is None else nn(step, chains[n])
            parents.append((a, b, coefs))
        level = parents
    coefs = level[0][2]
    for n in range(nodes):
        both = nn(chains[n], crossing[n][:, pair[n]])
        for j in (0, 1):
            k = 2 * n + j
            path[:, k * rank : (k + 1) * rank] = nt(both[:, j * rank : (j + 1) * rank], inner[k]) * weights[0, k].astype(f32)
    for n, leaf in enumerate(leaves):
        whole[:, pair[n]] = nn(coefs[:, n * rank : (n + 1) * rank], leaf)
    whole[:, count * rank :] = nt(nn(coefs, gram), coefs)


def top_kernel(whole, panel, top, sent, squares, held, sem):
    copy = pltpu.make_async_copy(panel, held, sem)
    copy.start()
    rank = whole.shape[0]
    depth = panel.shape[0]
    gram = whole[:, depth:]
    inverses, shrunk = shrink([gram])
    squares[:, :rank] = inverses[0]
    squares[:, rank:] = nn(shrunk[0], gram)
    copy.wait()
    factor = nn(whole[:, :depth], held[...])
    top[...] = factor
    sent[...] = nn(shrunk[0], factor)


def chip_kernel(place, own, partner, top, squares, tiles, tiles_core, step, near_out, tile_out, sketched, gram_out):
    rank, width = top.shape
    columns = width // 4
    step[...] = nn(squares[:, rank:] + nt_parts(partner[...], top[...]), squares[:, :rank])
    near = own[...] + partner[...]
    near_out[...] = near
    parts = [tiles[0], tiles_core[0], tiles[1], tiles_core[1]]
    sketched[...] = sum(part[:, columns : columns + rank] for part in parts)
    for k, part in enumerate(parts):
        tile_out[:, pl.ds(pl.multiple_of((place[0] ^ k) * columns, columns), columns)] = part[:, :columns]
    stack = jnp.concatenate([tile_out[...], near], axis=0)
    gram_out[...] = nt_parts(stack, stack)


def root_kernel(chunk, near, far, far_core, tile, gram_in, sketched, new_left, coefs_out):
    rank, width = tile.shape
    other = far[...] + far_core[...]
    cross = nt_parts(other, jnp.concatenate([tile[...], near[...], other], axis=0))
    above = jnp.concatenate([gram_in[...], cross[:, : 2 * rank].T], axis=1)
    gram = jnp.concatenate([above, cross], axis=0)
    parts = [slice(k * rank, (k + 1) * rank) for k in range(3)]
    inverses, shrunk = shrink([gram[s, s] for s in parts[1:]])
    both = jnp.concatenate(shrunk, axis=1)
    rows = nn(both, gram[rank:])
    inverse, last = shrink([nt(rows[:, rank:], both)])
    coefs = jnp.concatenate([sketched[...], -nn(last[0], both)], axis=1)
    final = nn(coefs, gram)
    down = nn(nt(final[:, rank:], both), inverse[0])
    steps = [-nn(nn(down, rows[:, s]), i) for s, i in zip(parts[1:], inverses)]
    _, factors = ridge_inverses([nt(final, coefs)])
    factor = factors[0]
    scale = float(width) ** 0.5
    columns = new_left.shape[1]
    here = pl.ds(pl.multiple_of(chunk[0] * columns, columns), columns)
    stack = jnp.concatenate([tile[:, here], near[:, here], far[:, here] + far_core[:, here]], axis=0)
    new_left[...] = nn(nn(factor, coefs) * scale, stack)
    coefs_out[...] = nn(factor, jnp.concatenate([final[:, parts[0]]] + steps, axis=1)) / scale


def copy_kernel(value, out):
    out[...] = value[...]


def right_kernel(*refs):
    paths, pieces, outs = refs[:4], refs[4:-4], refs[-4:]
    rank = paths[0].shape[0]
    stack = jnp.concatenate([path[...] for path in paths], axis=0)
    part = nn(stack, jnp.concatenate([piece[...] for piece in pieces], axis=1))
    for k, out in enumerate(outs):
        out[...] = part[k * rank : (k + 1) * rank]


def collect_kernel(spots, step, own, side, near, near_side, *refs):
    outs, held = refs[:4], refs[4]
    half = own.shape[1] // 2
    odd = spots[4] == 1
    k = 0
    for first, second in ((own, side), (near, near_side)):
        part = nn(step[...], jnp.concatenate([first[...], second[...]], axis=1))
        for i in range(2):
            a = part[:, i * half : (i + 1) * half]
            b = part[:, (2 + i) * half : (3 + i) * half]
            held[spots[k]] = jnp.concatenate([jnp.where(odd, b, a), jnp.where(odd, a, b)], axis=1)
            k += 1
    for k, out in enumerate(outs):
        out[...] = held[k]


def finish_kernel(coefs, tile, own, core, far, far_core, new_right):
    stack = jnp.concatenate([tile[...], own[...] + core[...], far[...] + far_core[...]], axis=0)
    new_right[...] = nn(coefs[...], stack)


def held(*shape):
    return pltpu.VMEM(shape, f32)


def call(kernel, out_shape, *operands, scalars=0, scratch=()):
    return pl.pallas_call(
        kernel,
        in_specs=[SMEM] * scalars + [VMEM] * (len(operands) - scalars),
        out_specs=jax.tree.map(lambda _: VMEM, out_shape, is_leaf=lambda v: not isinstance(v, list)),
        out_shape=out_shape,
        scratch_shapes=scratch,
        compiler_params=LIMIT,
        cost_estimate=SHORT,
    )(*operands)


def swap(value, axis, mask, members=None):
    members = range(lax.axis_size(axis)) if members is None else members
    return lax.ppermute(value, axis, [(i, i ^ mask) for i in members])


def chip_step(place, sent, top, squares, tiles, tiles_core):
    rank, width = top.shape
    core = swap(sent, "panels", 1)
    square, wide = held(rank, rank), held(rank, width)
    shapes = [square, wide, wide, square, held(2 * rank, 2 * rank)]
    return call(chip_kernel, shapes, place, sent, core, top, squares, tiles, tiles_core, scalars=1)


def gather_line(block, index, partial, tile, beside):
    ends, middle = (0, 1, 6, 7), (2, 3, 4, 5)
    is_end = (index < 2) | (index > 5)
    outward = [(2, 0), (3, 1), (4, 6), (5, 7)]

    near = swap(block, "rows", 2)
    center = swap(block, "rows", 6, middle)
    side = swap(block, "rows", 1)
    for mask in (1, 2):
        partial = partial + swap(partial, "rows", mask)
    outer = lax.ppermute(center, "rows", outward)
    near, center, side, partial, beside = lax.optimization_barrier((near, center, side, partial, beside))

    inner = swap(near, "rows", 6, middle)
    near_side = swap(near, "rows", 1)
    crossed = jnp.where(is_end, side, center)
    far_side = lax.ppermute(crossed, "rows", [(i, i ^ (6 if i in ends else 1)) for i in range(8)])
    outer, inner, near_side, far_side, partial, tile = lax.optimization_barrier(
        (outer, inner, near_side, far_side, partial, tile)
    )

    opposite = jnp.where(is_end, outer, inner)
    opposite, inner, partial = lax.optimization_barrier((opposite, inner, partial))
    far = lax.ppermute(inner, "rows", outward)
    opposite_side = swap(opposite, "rows", 1)
    partial = partial + swap(partial, "rows", 4)
    tiles = jnp.stack([tile, swap(tile, "panels", 2)])
    early = [block, side, near, near_side, opposite, far_side, center]
    late = [opposite_side, far]
    return [(v, index ^ k) for v, k in zip(early, (0, 1, 2, 3, 4, 7, 6))], [
        (v, index ^ k) for v, k in zip(late, (5, 6))
    ], partial, tiles, beside


def local(panel_left, panel_right, pivot_left, pivot_right, pattern, tile_left, tile_right, sketch):
    rows = lax.axis_size("rows")
    row = lax.axis_index("rows")
    place = lax.axis_index("panels")
    count, rank, local_columns = pivot_left.shape
    columns = tile_left.shape[2]
    width = panel_left.shape[3]
    wide = held(rank, width)
    square = held(rank, rank)
    chunk = held(rank, columns)
    tile_left, tile_right = tile_left[0], tile_right[0]
    spot = place.reshape(1).astype(jnp.int32)

    sketch_here = lax.dynamic_slice_in_dim(sketch, row * local_columns, local_columns, 1)
    sketched = jnp.einsum("rb,jkb->jrk", sketch_here, pivot_left, precision=highest)
    sketch_tile = lax.dynamic_slice_in_dim(sketch, place * columns, columns, 1)
    tile_sketched = nt(sketch_tile, tile_right)
    panel = panel_left.reshape(count * rank, width)
    products = nt(panel, panel)
    routed = rows == 8 and local_columns % 128 == 0
    tile = jnp.concatenate([tile_left, tile_sketched, jnp.zeros_like(tile_sketched)], axis=1)
    if routed:
        early, late, sketched, tiles, products = gather_line(pivot_right, row, sketched, tile, products)
    else:
        sketched = lax.psum(sketched, "rows")
        tiles = jnp.stack([tile, swap(tile, "panels", 2)])

    if routed:
        inner = inner_products(panel_right, [v for v, _ in early], [s for _, s in early])
        inner, sketched, tiles = lax.optimization_barrier((inner, sketched, tiles))
        _, pivot_left, tiles = lax.optimization_barrier((late, pivot_left, tiles))
        pivot = call(copy_kernel, held(count * rank, local_columns), pivot_left.reshape(count * rank, local_columns))
        inner, pivot = lax.optimization_barrier((inner, pivot))
        opposite = swap(pivot, "rows", 4)
        inner = inner_products(panel_right, [v for v, _ in late], [s for _, s in late], inner)
    else:
        full = lax.all_gather(pivot_right, "rows", axis=2, tiled=True)
        inner = inner_products(panel_right, [full], [jnp.int32(0)])
    tiles_core = swap(tiles, "panels", 1)

    path, whole = call(
        tree_kernel,
        [held(rank, count * rank), held(rank, (count + 1) * rank)],
        pattern,
        sketched,
        inner,
        products,
        scalars=1,
    )
    top, sent, squares = pl.pallas_call(
        top_kernel,
        in_specs=[VMEM, pl.BlockSpec(memory_space=pl.ANY)],
        out_specs=[VMEM] * 3,
        out_shape=[wide, wide, held(rank, 2 * rank)],
        scratch_shapes=[pltpu.VMEM(panel.shape, f32), pltpu.SemaphoreType.DMA],
        compiler_params=ROOMY,
        cost_estimate=SHORT,
    )(whole, panel)
    if routed:
        pieces = [pivot, opposite]
        paths = [path] + [swap(path, "rows", mask) for mask in (1, 2, 3)]
        half = held(rank, 2 * local_columns)
        paths, pieces, sent = lax.optimization_barrier((paths, pieces, sent))
        far = swap(sent, "panels", 2)
        step, near, whole_tile, tile_sketched, gram = chip_step(spot, sent, top, squares, tiles, tiles_core)
        mine, *given = call(right_kernel, [half] * 4, *paths, *pieces)
        got = [mine] + [swap(v, "rows", mask) for mask, v in zip((1, 2, 3), given)]
        depth = row // 2
        spots = jnp.stack([depth ^ place, depth ^ 2 ^ place, depth ^ 1 ^ place, depth ^ 3 ^ place, row % 2])
        parts = call(collect_kernel, [chunk] * 4, spots.astype(jnp.int32), step, *got, scalars=1, scratch=[pltpu.VMEM((4, rank, columns), f32)])
        far, own_part = lax.optimization_barrier((far, parts[0]))
        rights = [own_part] + [swap(parts[mask], "panels", mask) for mask in (1, 2, 3)]
    else:
        step, near, whole_tile, tile_sketched, gram = chip_step(spot, sent, top, squares, tiles, tiles_core)
        far = swap(sent, "panels", 2)
        full_left = lax.all_gather(pivot_left, "rows", axis=2, tiled=True)
        right = nn(step, nn(path, full_left.reshape(count * rank, width)))
        rights = []
        for mask in range(4):
            part = lax.dynamic_slice_in_dim(right, (place ^ mask) * columns, columns, 1)
            rights.append(swap(part, "panels", mask) if mask else part)

    far_core = swap(far, "panels", 1)
    new_left, coefs = call(
        root_kernel,
        [jax.ShapeDtypeStruct((rank, columns), f32), held(rank, 3 * rank)],
        spot,
        near,
        far,
        far_core,
        whole_tile,
        gram,
        tile_sketched,
        scalars=1,
    )
    new_right = call(finish_kernel, jax.ShapeDtypeStruct((rank, columns), f32), coefs, tile_right, *rights)
    return (new_left[None], new_right[None])


def solution(mesh):
    return jax.shard_map(
        local,
        mesh=mesh,
        in_specs=(
            P("rows", "panels", None, None),
            P("rows", "panels", None, None),
            P("panels", None, "rows"),
            P("panels", None, "rows"),
            P("rows", "panels"),
            P("rows", None, "panels"),
            P("rows", None, "panels"),
            P(),
        ),
        out_specs=(P("rows", None, "panels"), P("rows", None, "panels")),
        check_vma=False,
    )
```

```python
import functools

import jax
import jax.numpy as jnp
from jax import lax
from jax.experimental import pallas as pl
from jax.experimental.pallas import tpu as pltpu
from jax.sharding import PartitionSpec as P

highest = lax.Precision.HIGHEST
f32 = jnp.float32
VMEM = pl.BlockSpec(memory_space=pltpu.VMEM)
SMEM = pl.BlockSpec(memory_space=pltpu.SMEM)
LIMIT = pltpu.CompilerParams(vmem_limit_bytes=12 * 1024 * 1024)
ROOMY = pltpu.CompilerParams(vmem_limit_bytes=20 * 1024 * 1024)
SHORT = pl.CostEstimate(flops=10**8, bytes_accessed=10**6, transcendentals=0)


def dot(a, b, dims):
    return lax.dot_general(a, b, (dims, ((), ())), precision=highest, preferred_element_type=f32)


def nn(a, b):
    return dot(a, b, ((1,), (0,)))


def nt(a, b):
    return dot(a, b, ((1,), (1,)))


def tn(a, b):
    return dot(a, b, ((0,), (0,)))


def identity(n):
    return (lax.broadcasted_iota(jnp.int32, (n, n), 0) == lax.broadcasted_iota(jnp.int32, (n, n), 1)).astype(f32)


def inverse_factors(matrices):
    n = matrices[0].shape[0]
    step = 8 if len(matrices) < 3 else 4
    eye = identity(n)
    states = []
    for matrix in matrices:
        both = jnp.concatenate([matrix, eye], axis=1)
        states.append([both[8 * m : 8 * m + 8] for m in range(n // 8)])
    sub = lax.broadcasted_iota(jnp.int32, (8, 2 * n), 0)
    for k in range(0, n, step):
        m, s = k // 8, k % 8
        for state in states:
            row = [state[m][s + a : s + a + 1] for a in range(step)]
            pivot = [
                [jnp.broadcast_to(row[a][:, k + b : k + b + 1], (1, 2 * n)) if b >= a else None for b in range(step)]
                for a in range(step)
            ]
            rest = [t for t in range(m, n // 8) if not (t == m and s + step == 8)]
            column = [{t: jnp.broadcast_to(state[t][:, k + b : k + b + 1], (8, 2 * n)) for t in rest} for b in range(step)]
            if m in rest:
                for b in range(step):
                    column[b][m] = jnp.where(sub >= s + step, column[b][m], 0.0)
            done = state[m]
            scaled = []
            for a in range(step):
                inverse = 1.0 / pivot[a][a]
                for b in range(a + 1, step):
                    factor = pivot[a][b] * inverse
                    row[b] = row[b] - factor * row[a]
                    for c in range(b, step):
                        pivot[b][c] = pivot[b][c] - factor * pivot[a][c]
                    for t in rest:
                        column[b][t] = column[b][t] - column[a][t] * factor
                scaled.append(row[a] * inverse)
                done = jnp.where(sub == s + a, row[a] * lax.rsqrt(pivot[a][a]), done)
            state[m] = done
            for t in rest:
                total = state[t]
                for a in range(step):
                    total = total - column[a][t] * scaled[a]
                state[t] = total
    return [jnp.concatenate([block[:, n:] for block in state], axis=0) for state in states]


def ridge_inverses(grams):
    n = grams[0].shape[0]
    eye = identity(n)
    ridges = [0.001 * jnp.sum(jnp.sum(g * eye, axis=1, keepdims=True), axis=0, keepdims=True) / n + 1e-06 for g in grams]
    factors = inverse_factors([g + e * eye for g, e in zip(grams, ridges)])
    return ridges, factors


def shrink(grams):
    eye = identity(grams[0].shape[0])
    ridges, factors = ridge_inverses(grams)
    inverses = [tn(c, c) for c in factors]
    return inverses, [eye - e * s for e, s in zip(ridges, inverses)]


def split(value):
    parts = []
    for _ in range(3):
        part = value.astype(jnp.bfloat16)
        parts.append(part)
        value = value - part.astype(f32)
    return parts


def nt_parts(a, b):
    m, n = a.shape[0], b.shape[0]
    stacked = lax.dot_general(
        jnp.concatenate(split(a), axis=0),
        jnp.concatenate(split(b), axis=0),
        (((1,), (1,)), ((), ())),
        preferred_element_type=f32,
    )

    def block(i, k):
        return stacked[i * m : (i + 1) * m, k * n : (k + 1) * n]

    small = block(1, 1) + block(0, 2) + block(2, 0)
    return block(0, 0) + (block(0, 1) + block(1, 0) + small)


def inner_kernel(count, *refs):
    panels, pieces, add, out = refs[1 : 1 + count], refs[1 + count : 1 + 2 * count], refs[1 + 2 * count : -1], refs[-1]
    for j in range(out.shape[0]):
        left = jnp.concatenate([piece[j] for piece in pieces], axis=1)
        right = jnp.concatenate([panel[0, j] for panel in panels], axis=1)
        term = nt_parts(left, right)
        out[j] = term + add[0][j] if add else term


def inner_products(panel_right, pieces, sources, add=None):
    count = len(pieces)
    _, j, rank, _ = panel_right.shape
    width = pieces[0].shape[2]
    group = j // 2
    square = pl.BlockSpec((group, rank, rank), lambda i, s: (i, 0, 0))
    in_specs = [pl.BlockSpec((1, group, rank, width), functools.partial(lambda i, s, k: (0, i, 0, s[k]), k=k)) for k in range(count)]
    in_specs += [pl.BlockSpec((group, rank, width), lambda i, s: (i, 0, 0))] * count
    in_specs += [square] if add is not None else []
    return pl.pallas_call(
        functools.partial(inner_kernel, count),
        grid_spec=pltpu.PrefetchScalarGridSpec(num_scalar_prefetch=1, grid=(j // group,), in_specs=in_specs, out_specs=square),
        out_shape=held(j, rank, rank),
        compiler_params=ROOMY,
        cost_estimate=SHORT,
    )(jnp.stack(sources).astype(jnp.int32), *([panel_right] * count), *pieces, *([] if add is None else [add]))


def tree_kernel(weights, sketched, inner, products, path, whole):
    count, rank, _ = sketched.shape
    nodes = count // 2
    leaves = [
        jnp.concatenate([nn(sketched[j], inner[j]) * weights[0, j].astype(f32) for j in (2 * n, 2 * n + 1)], axis=1)
        for n in range(nodes)
    ]
    pair = [slice(2 * n * rank, 2 * (n + 1) * rank) for n in range(nodes)]
    crossing = [nn(leaf, products[s]) for leaf, s in zip(leaves, pair)]
    crossing_all = jnp.concatenate(crossing, axis=0)
    gram = jnp.concatenate([nt(crossing_all[:, s], leaf) for leaf, s in zip(leaves, pair)], axis=1)
    chains = [None] * nodes
    level = [(n, n + 1, None) for n in range(nodes)]

    def times(coefs, matrix):
        return matrix if coefs is None else nn(coefs, matrix)

    def times_t(matrix, coefs):
        return matrix if coefs is None else nt(matrix, coefs)

    def after(matrix, coefs):
        return matrix if coefs is None else nn(matrix, coefs)

    while len(level) > 1:
        spans = [slice(a * rank, b * rank) for a, b, _ in level]
        crossed = [times(h, gram[s]) for (_, _, h), s in zip(level, spans)]
        inverses, shrunk = shrink([times_t(x[:, s], h) for x, s, (_, _, h) in zip(crossed, spans, level)])
        parents = []
        for m in range(0, len(level), 2):
            (a, _, ha), (_, b, hb) = level[m], level[m + 1]
            coefs = jnp.concatenate([after(shrunk[m], ha), after(shrunk[m + 1], hb)], axis=1)
            rows = nn(coefs, gram[a * rank : b * rank])
            for child in (m, m + 1):
                first, last, h = level[child]
                step = nn(times_t(rows[:, spans[child]], h), inverses[child])
                for n in range(first, last):
                    chains[n] = step if chains[n] is None else nn(step, chains[n])
            parents.append((a, b, coefs))
        level = parents
    coefs = level[0][2]
    for n in range(nodes):
        both = nn(chains[n], crossing[n][:, pair[n]])
        for j in (0, 1):
            k = 2 * n + j
            path[:, k * rank : (k + 1) * rank] = nt(both[:, j * rank : (j + 1) * rank], inner[k]) * weights[0, k].astype(f32)
    for n, leaf in enumerate(leaves):
        whole[:, pair[n]] = nn(coefs[:, n * rank : (n + 1) * rank], leaf)
    whole[:, count * rank :] = nt(nn(coefs, gram), coefs)


def top_kernel(whole, panel, top, sent, squares, held, sem):
    copy = pltpu.make_async_copy(panel, held, sem)
    copy.start()
    rank = whole.shape[0]
    depth = panel.shape[0]
    gram = whole[:, depth:]
    inverses, shrunk = shrink([gram])
    squares[:, :rank] = inverses[0]
    squares[:, rank:] = nn(shrunk[0], gram)
    copy.wait()
    factor = nn(whole[:, :depth], held[...])
    top[...] = factor
    sent[...] = nn(shrunk[0], factor)


def chip_kernel(place, own, partner, top, squares, tiles, tiles_core, step, near_out, tile_out, sketched, gram_out):
    rank, width = top.shape
    columns = width // 4
    step[...] = nn(squares[:, rank:] + nt_parts(partner[...], top[...]), squares[:, :rank])
    near = own[...] + partner[...]
    near_out[...] = near
    parts = [tiles[0], tiles_core[0], tiles[1], tiles_core[1]]
    sketched[...] = sum(part[:, columns : columns + rank] for part in parts)
    for k, part in enumerate(parts):
        tile_out[:, pl.ds(pl.multiple_of((place[0] ^ k) * columns, columns), columns)] = part[:, :columns]
    stack = jnp.concatenate([tile_out[...], near], axis=0)
    gram_out[...] = nt_parts(stack, stack)


def root_kernel(chunk, near, far, far_core, tile, gram_in, sketched, new_left, coefs_out):
    rank, width = tile.shape
    other = far[...] + far_core[...]
    cross = nt_parts(other, jnp.concatenate([tile[...], near[...], other], axis=0))
    above = jnp.concatenate([gram_in[...], cross[:, : 2 * rank].T], axis=1)
    gram = jnp.concatenate([above, cross], axis=0)
    parts = [slice(k * rank, (k + 1) * rank) for k in range(3)]
    inverses, shrunk = shrink([gram[s, s] for s in parts[1:]])
    both = jnp.concatenate(shrunk, axis=1)
    rows = nn(both, gram[rank:])
    inverse, last = shrink([nt(rows[:, rank:], both)])
    coefs = jnp.concatenate([sketched[...], -nn(last[0], both)], axis=1)
    final = nn(coefs, gram)
    down = nn(nt(final[:, rank:], both), inverse[0])
    steps = [-nn(nn(down, rows[:, s]), i) for s, i in zip(parts[1:], inverses)]
    _, factors = ridge_inverses([nt(final, coefs)])
    factor = factors[0]
    scale = float(width) ** 0.5
    columns = new_left.shape[1]
    here = pl.ds(pl.multiple_of(chunk[0] * columns, columns), columns)
    stack = jnp.concatenate([tile[:, here], near[:, here], far[:, here] + far_core[:, here]], axis=0)
    new_left[...] = nn(nn(factor, coefs) * scale, stack)
    coefs_out[...] = nn(factor, jnp.concatenate([final[:, parts[0]]] + steps, axis=1)) / scale


def copy_kernel(value, out):
    out[...] = value[...]


def right_kernel(*refs):
    paths, pieces, outs = refs[:4], refs[4:-4], refs[-4:]
    rank = paths[0].shape[0]
    stack = jnp.concatenate([path[...] for path in paths], axis=0)
    part = nn(stack, jnp.concatenate([piece[...] for piece in pieces], axis=1))
    for k, out in enumerate(outs):
        out[...] = part[k * rank : (k + 1) * rank]


def collect_kernel(spots, step, own, side, near, near_side, *refs):
    outs, held = refs[:4], refs[4]
    half = own.shape[1] // 2
    odd = spots[4] == 1
    k = 0
    for first, second in ((own, side), (near, near_side)):
        part = nn(step[...], jnp.concatenate([first[...], second[...]], axis=1))
        for i in range(2):
            a = part[:, i * half : (i + 1) * half]
            b = part[:, (2 + i) * half : (3 + i) * half]
            held[spots[k]] = jnp.concatenate([jnp.where(odd, b, a), jnp.where(odd, a, b)], axis=1)
            k += 1
    for k, out in enumerate(outs):
        out[...] = held[k]


def finish_kernel(coefs, tile, own, core, far, far_core, new_right):
    stack = jnp.concatenate([tile[...], own[...] + core[...], far[...] + far_core[...]], axis=0)
    new_right[...] = nn(coefs[...], stack)


def held(*shape):
    return pltpu.VMEM(shape, f32)


def call(kernel, out_shape, *operands, scalars=0, scratch=()):
    return pl.pallas_call(
        kernel,
        in_specs=[SMEM] * scalars + [VMEM] * (len(operands) - scalars),
        out_specs=jax.tree.map(lambda _: VMEM, out_shape, is_leaf=lambda v: not isinstance(v, list)),
        out_shape=out_shape,
        scratch_shapes=scratch,
        compiler_params=LIMIT,
        cost_estimate=SHORT,
    )(*operands)


def swap(value, axis, mask, members=None):
    members = range(lax.axis_size(axis)) if members is None else members
    return lax.ppermute(value, axis, [(i, i ^ mask) for i in members])


def chip_step(place, sent, top, squares, tiles, tiles_core):
    rank, width = top.shape
    core = swap(sent, "panels", 1)
    square, wide = held(rank, rank), held(rank, width)
    shapes = [square, wide, wide, square, held(2 * rank, 2 * rank)]
    return call(chip_kernel, shapes, place, sent, core, top, squares, tiles, tiles_core, scalars=1)


def gather_line(block, index, partial, tile, beside):
    ends, middle = (0, 1, 6, 7), (2, 3, 4, 5)
    is_end = (index < 2) | (index > 5)
    outward = [(2, 0), (3, 1), (4, 6), (5, 7)]

    near = swap(block, "rows", 2)
    center = swap(block, "rows", 6, middle)
    side = swap(block, "rows", 1)
    for mask in (1, 2):
        partial = partial + swap(partial, "rows", mask)
    outer = lax.ppermute(center, "rows", outward)
    near, center, side, partial, beside = lax.optimization_barrier((near, center, side, partial, beside))

    inner = swap(near, "rows", 6, middle)
    near_side = swap(near, "rows", 1)
    crossed = jnp.where(is_end, side, center)
    far_side = lax.ppermute(crossed, "rows", [(i, i ^ (6 if i in ends else 1)) for i in range(8)])
    outer, inner, near_side, far_side, partial, tile = lax.optimization_barrier(
        (outer, inner, near_side, far_side, partial, tile)
    )

    opposite = jnp.where(is_end, outer, inner)
    far = lax.ppermute(inner, "rows", outward)
    opposite_side = swap(opposite, "rows", 1)
    partial = partial + swap(partial, "rows", 4)
    tiles = jnp.stack([tile, swap(tile, "panels", 2)])
    early = [block, side, near, near_side, opposite, far_side, center]
    late = [opposite_side, far]
    return [(v, index ^ k) for v, k in zip(early, (0, 1, 2, 3, 4, 7, 6))], [
        (v, index ^ k) for v, k in zip(late, (5, 6))
    ], partial, tiles, beside


def local(panel_left, panel_right, pivot_left, pivot_right, pattern, tile_left, tile_right, sketch):
    rows = lax.axis_size("rows")
    row = lax.axis_index("rows")
    place = lax.axis_index("panels")
    count, rank, local_columns = pivot_left.shape
    columns = tile_left.shape[2]
    width = panel_left.shape[3]
    wide = held(rank, width)
    square = held(rank, rank)
    chunk = held(rank, columns)
    tile_left, tile_right = tile_left[0], tile_right[0]
    spot = place.reshape(1).astype(jnp.int32)

    sketch_here = lax.dynamic_slice_in_dim(sketch, row * local_columns, local_columns, 1)
    sketched = jnp.einsum("rb,jkb->jrk", sketch_here, pivot_left, precision=highest)
    sketch_tile = lax.dynamic_slice_in_dim(sketch, place * columns, columns, 1)
    tile_sketched = nt(sketch_tile, tile_right)
    panel = panel_left.reshape(count * rank, width)
    products = nt(panel, panel)
    routed = rows == 8 and local_columns % 128 == 0
    tile = jnp.concatenate([tile_left, tile_sketched, jnp.zeros_like(tile_sketched)], axis=1)
    if routed:
        early, late, sketched, tiles, products = gather_line(pivot_right, row, sketched, tile, products)
    else:
        sketched = lax.psum(sketched, "rows")
        tiles = jnp.stack([tile, swap(tile, "panels", 2)])

    if routed:
        inner = inner_products(panel_right, [v for v, _ in early], [s for _, s in early])
        inner, sketched, tiles = lax.optimization_barrier((inner, sketched, tiles))
        _, pivot_left, tiles = lax.optimization_barrier((late, pivot_left, tiles))
        pivot = call(copy_kernel, held(count * rank, local_columns), pivot_left.reshape(count * rank, local_columns))
        inner, pivot = lax.optimization_barrier((inner, pivot))
        opposite = swap(pivot, "rows", 4)
        inner = inner_products(panel_right, [v for v, _ in late], [s for _, s in late], inner)
    else:
        full = lax.all_gather(pivot_right, "rows", axis=2, tiled=True)
        inner = inner_products(panel_right, [full], [jnp.int32(0)])
    tiles_core = swap(tiles, "panels", 1)

    path, whole = call(
        tree_kernel,
        [held(rank, count * rank), held(rank, (count + 1) * rank)],
        pattern,
        sketched,
        inner,
        products,
        scalars=1,
    )
    top, sent, squares = pl.pallas_call(
        top_kernel,
        in_specs=[VMEM, pl.BlockSpec(memory_space=pl.ANY)],
        out_specs=[VMEM] * 3,
        out_shape=[wide, wide, held(rank, 2 * rank)],
        scratch_shapes=[pltpu.VMEM(panel.shape, f32), pltpu.SemaphoreType.DMA],
        compiler_params=ROOMY,
        cost_estimate=SHORT,
    )(whole, panel)
    if routed:
        pieces = [pivot, opposite]
        paths = [path] + [swap(path, "rows", mask) for mask in (1, 2, 3)]
        half = held(rank, 2 * local_columns)
        paths, pieces, sent = lax.optimization_barrier((paths, pieces, sent))
        far = swap(sent, "panels", 2)
        step, near, whole_tile, tile_sketched, gram = chip_step(spot, sent, top, squares, tiles, tiles_core)
        mine, *given = call(right_kernel, [half] * 4, *paths, *pieces)
        got = [mine] + [swap(v, "rows", mask) for mask, v in zip((1, 2, 3), given)]
        depth = row // 2
        spots = jnp.stack([depth ^ place, depth ^ 2 ^ place, depth ^ 1 ^ place, depth ^ 3 ^ place, row % 2])
        parts = call(collect_kernel, [chunk] * 4, spots.astype(jnp.int32), step, *got, scalars=1, scratch=[pltpu.VMEM((4, rank, columns), f32)])
        far, own_part = lax.optimization_barrier((far, parts[0]))
        rights = [own_part] + [swap(parts[mask], "panels", mask) for mask in (1, 2, 3)]
    else:
        step, near, whole_tile, tile_sketched, gram = chip_step(spot, sent, top, squares, tiles, tiles_core)
        far = swap(sent, "panels", 2)
        full_left = lax.all_gather(pivot_left, "rows", axis=2, tiled=True)
        right = nn(step, nn(path, full_left.reshape(count * rank, width)))
        rights = []
        for mask in range(4):
            part = lax.dynamic_slice_in_dim(right, (place ^ mask) * columns, columns, 1)
            rights.append(swap(part, "panels", mask) if mask else part)

    far_core = swap(far, "panels", 1)
    new_left, coefs = call(
        root_kernel,
        [jax.ShapeDtypeStruct((rank, columns), f32), held(rank, 3 * rank)],
        spot,
        near,
        far,
        far_core,
        whole_tile,
        gram,
        tile_sketched,
        scalars=1,
    )
    new_right = call(finish_kernel, jax.ShapeDtypeStruct((rank, columns), f32), coefs, tile_right, *rights)
    return (new_left[None], new_right[None])


def solution(mesh):
    return jax.shard_map(
        local,
        mesh=mesh,
        in_specs=(
            P("rows", "panels", None, None),
            P("rows", "panels", None, None),
            P("panels", None, "rows"),
            P("panels", None, "rows"),
            P("rows", "panels"),
            P("rows", None, "panels"),
            P("rows", None, "panels"),
            P(),
        ),
        out_specs=(P("rows", None, "panels"), P("rows", None, "panels")),
        check_vma=False,
    )
```

```python
import functools

import jax
import jax.numpy as jnp
from jax import lax
from jax.experimental import pallas as pl
from jax.experimental.pallas import tpu as pltpu
from jax.sharding import PartitionSpec as P

highest = lax.Precision.HIGHEST
f32 = jnp.float32
VMEM = pl.BlockSpec(memory_space=pltpu.VMEM)
SMEM = pl.BlockSpec(memory_space=pltpu.SMEM)
LIMIT = pltpu.CompilerParams(vmem_limit_bytes=12 * 1024 * 1024)
ROOMY = pltpu.CompilerParams(vmem_limit_bytes=20 * 1024 * 1024)
SHORT = pl.CostEstimate(flops=10**8, bytes_accessed=10**6, transcendentals=0)


def dot(a, b, dims):
    return lax.dot_general(a, b, (dims, ((), ())), precision=highest, preferred_element_type=f32)


def nn(a, b):
    return dot(a, b, ((1,), (0,)))


def nt(a, b):
    return dot(a, b, ((1,), (1,)))


def tn(a, b):
    return dot(a, b, ((0,), (0,)))


def identity(n):
    return (lax.broadcasted_iota(jnp.int32, (n, n), 0) == lax.broadcasted_iota(jnp.int32, (n, n), 1)).astype(f32)


def inverse_factors(matrices):
    n = matrices[0].shape[0]
    step = 8 if len(matrices) < 3 else 4
    eye = identity(n)
    states = []
    for matrix in matrices:
        both = jnp.concatenate([matrix, eye], axis=1)
        states.append([both[8 * m : 8 * m + 8] for m in range(n // 8)])
    sub = lax.broadcasted_iota(jnp.int32, (8, 2 * n), 0)
    for k in range(0, n, step):
        m, s = k // 8, k % 8
        for state in states:
            row = [state[m][s + a : s + a + 1] for a in range(step)]
            pivot = [
                [jnp.broadcast_to(row[a][:, k + b : k + b + 1], (1, 2 * n)) if b >= a else None for b in range(step)]
                for a in range(step)
            ]
            rest = [t for t in range(m, n // 8) if not (t == m and s + step == 8)]
            column = [{t: jnp.broadcast_to(state[t][:, k + b : k + b + 1], (8, 2 * n)) for t in rest} for b in range(step)]
            if m in rest:
                for b in range(step):
                    column[b][m] = jnp.where(sub >= s + step, column[b][m], 0.0)
            done = state[m]
            scaled = []
            for a in range(step):
                inverse = 1.0 / pivot[a][a]
                for b in range(a + 1, step):
                    factor = pivot[a][b] * inverse
                    row[b] = row[b] - factor * row[a]
                    for c in range(b, step):
                        pivot[b][c] = pivot[b][c] - factor * pivot[a][c]
                    for t in rest:
                        column[b][t] = column[b][t] - column[a][t] * factor
                scaled.append(row[a] * inverse)
                done = jnp.where(sub == s + a, row[a] * lax.rsqrt(pivot[a][a]), done)
            state[m] = done
            for t in rest:
                total = state[t]
                for a in range(step):
                    total = total - column[a][t] * scaled[a]
                state[t] = total
    return [jnp.concatenate([block[:, n:] for block in state], axis=0) for state in states]


def ridge_inverses(grams):
    n = grams[0].shape[0]
    eye = identity(n)
    ridges = [0.001 * jnp.sum(jnp.sum(g * eye, axis=1, keepdims=True), axis=0, keepdims=True) / n + 1e-06 for g in grams]
    factors = inverse_factors([g + e * eye for g, e in zip(grams, ridges)])
    return ridges, factors


def shrink(grams):
    eye = identity(grams[0].shape[0])
    ridges, factors = ridge_inverses(grams)
    inverses = [tn(c, c) for c in factors]
    return inverses, [eye - e * s for e, s in zip(ridges, inverses)]


def split(value):
    parts = []
    for _ in range(3):
        part = value.astype(jnp.bfloat16)
        parts.append(part)
        value = value - part.astype(f32)
    return parts


def nt_parts(a, b):
    m, n = a.shape[0], b.shape[0]
    stacked = lax.dot_general(
        jnp.concatenate(split(a), axis=0),
        jnp.concatenate(split(b), axis=0),
        (((1,), (1,)), ((), ())),
        preferred_element_type=f32,
    )

    def block(i, k):
        return stacked[i * m : (i + 1) * m, k * n : (k + 1) * n]

    small = block(1, 1) + block(0, 2) + block(2, 0)
    return block(0, 0) + (block(0, 1) + block(1, 0) + small)


def nn_parts(a, b):
    m = a.shape[0]
    one, two, three = split(a)
    none = jnp.zeros_like(one)
    left = [[one, one, one], [two, two, none], [three, none, none]]
    stacked = lax.dot_general(
        jnp.concatenate([jnp.concatenate(row, axis=1) for row in left], axis=0),
        jnp.concatenate(split(b), axis=0),
        (((1,), (0,)), ((), ())),
        preferred_element_type=f32,
    )
    return stacked[:m] + (stacked[m : 2 * m] + stacked[2 * m :])


def inner_kernel(count, *refs):
    panels, pieces, add, out = refs[1 : 1 + count], refs[1 + count : 1 + 2 * count], refs[1 + 2 * count : -1], refs[-1]
    for j in range(out.shape[0]):
        left = jnp.concatenate([piece[j] for piece in pieces], axis=1)
        right = jnp.concatenate([panel[0, j] for panel in panels], axis=1)
        term = nt_parts(left, right)
        out[j] = term + add[0][j] if add else term


def inner_products(panel_right, pieces, sources, add=None):
    count = len(pieces)
    _, j, rank, _ = panel_right.shape
    width = pieces[0].shape[2]
    group = j // 2
    square = pl.BlockSpec((group, rank, rank), lambda i, s: (i, 0, 0))
    in_specs = [pl.BlockSpec((1, group, rank, width), functools.partial(lambda i, s, k: (0, i, 0, s[k]), k=k)) for k in range(count)]
    in_specs += [pl.BlockSpec((group, rank, width), lambda i, s: (i, 0, 0))] * count
    in_specs += [square] if add is not None else []
    return pl.pallas_call(
        functools.partial(inner_kernel, count),
        grid_spec=pltpu.PrefetchScalarGridSpec(num_scalar_prefetch=1, grid=(j // group,), in_specs=in_specs, out_specs=square),
        out_shape=held(j, rank, rank),
        compiler_params=ROOMY,
        cost_estimate=SHORT,
    )(jnp.stack(sources).astype(jnp.int32), *([panel_right] * count), *pieces, *([] if add is None else [add]))


def tree_kernel(weights, sketched, inner, products, path, whole):
    count, rank, _ = sketched.shape
    nodes = count // 2
    leaves = [
        jnp.concatenate([nn(sketched[j], inner[j]) * weights[0, j].astype(f32) for j in (2 * n, 2 * n + 1)], axis=1)
        for n in range(nodes)
    ]
    pair = [slice(2 * n * rank, 2 * (n + 1) * rank) for n in range(nodes)]
    crossing = [nn(leaf, products[s]) for leaf, s in zip(leaves, pair)]
    crossing_all = jnp.concatenate(crossing, axis=0)
    gram = jnp.concatenate([nt(crossing_all[:, s], leaf) for leaf, s in zip(leaves, pair)], axis=1)
    chains = [None] * nodes
    level = [(n, n + 1, None) for n in range(nodes)]

    def times(coefs, matrix):
        return matrix if coefs is None else nn(coefs, matrix)

    def times_t(matrix, coefs):
        return matrix if coefs is None else nt(matrix, coefs)

    def after(matrix, coefs):
        return matrix if coefs is None else nn(matrix, coefs)

    while len(level) > 1:
        spans = [slice(a * rank, b * rank) for a, b, _ in level]
        crossed = [times(h, gram[s]) for (_, _, h), s in zip(level, spans)]
        inverses, shrunk = shrink([times_t(x[:, s], h) for x, s, (_, _, h) in zip(crossed, spans, level)])
        parents = []
        for m in range(0, len(level), 2):
            (a, _, ha), (_, b, hb) = level[m], level[m + 1]
            coefs = jnp.concatenate([after(shrunk[m], ha), after(shrunk[m + 1], hb)], axis=1)
            rows = nn(coefs, gram[a * rank : b * rank])
            for child in (m, m + 1):
                first, last, h = level[child]
                step = nn(times_t(rows[:, spans[child]], h), inverses[child])
                for n in range(first, last):
                    chains[n] = step if chains[n] is None else nn(step, chains[n])
            parents.append((a, b, coefs))
        level = parents
    coefs = level[0][2]
    for n in range(nodes):
        both = nn(chains[n], crossing[n][:, pair[n]])
        for j in (0, 1):
            k = 2 * n + j
            path[:, k * rank : (k + 1) * rank] = nt(both[:, j * rank : (j + 1) * rank], inner[k]) * weights[0, k].astype(f32)
    for n, leaf in enumerate(leaves):
        whole[:, pair[n]] = nn(coefs[:, n * rank : (n + 1) * rank], leaf)
    whole[:, count * rank :] = nt(nn(coefs, gram), coefs)


def top_kernel(whole, panel, top, sent, squares, held, sem):
    copy = pltpu.make_async_copy(panel, held, sem)
    copy.start()
    rank = whole.shape[0]
    depth = panel.shape[0]
    gram = whole[:, depth:]
    inverses, shrunk = shrink([gram])
    squares[:, :rank] = inverses[0]
    squares[:, rank:] = nn(shrunk[0], gram)
    copy.wait()
    factor = nn(whole[:, :depth], held[...])
    top[...] = factor
    sent[...] = nn_parts(shrunk[0], factor)


def chip_kernel(place, own, partner, top, squares, tiles, tiles_core, step, near_out, tile_out, sketched, gram_out):
    rank, width = top.shape
    columns = width // 4
    step[...] = nn(squares[:, rank:] + nt_parts(partner[...], top[...]), squares[:, :rank])
    near = own[...] + partner[...]
    near_out[...] = near
    parts = [tiles[0], tiles_core[0], tiles[1], tiles_core[1]]
    sketched[...] = sum(part[:, columns : columns + rank] for part in parts)
    for k, part in enumerate(parts):
        tile_out[:, pl.ds(pl.multiple_of((place[0] ^ k) * columns, columns), columns)] = part[:, :columns]
    stack = jnp.concatenate([tile_out[...], near], axis=0)
    gram_out[...] = nt_parts(stack, stack)


def root_kernel(chunk, near, far, far_core, tile, gram_in, sketched, new_left, coefs_out):
    rank, width = tile.shape
    other = far[...] + far_core[...]
    cross = nt_parts(other, jnp.concatenate([tile[...], near[...], other], axis=0))
    above = jnp.concatenate([gram_in[...], cross[:, : 2 * rank].T], axis=1)
    gram = jnp.concatenate([above, cross], axis=0)
    parts = [slice(k * rank, (k + 1) * rank) for k in range(3)]
    inverses, shrunk = shrink([gram[s, s] for s in parts[1:]])
    both = jnp.concatenate(shrunk, axis=1)
    rows = nn(both, gram[rank:])
    inverse, last = shrink([nt(rows[:, rank:], both)])
    coefs = jnp.concatenate([sketched[...], -nn(last[0], both)], axis=1)
    final = nn(coefs, gram)
    down = nn(nt(final[:, rank:], both), inverse[0])
    steps = [-nn(nn(down, rows[:, s]), i) for s, i in zip(parts[1:], inverses)]
    _, factors = ridge_inverses([nt(final, coefs)])
    factor = factors[0]
    scale = float(width) ** 0.5
    columns = new_left.shape[1]
    here = pl.ds(pl.multiple_of(chunk[0] * columns, columns), columns)
    stack = jnp.concatenate([tile[:, here], near[:, here], far[:, here] + far_core[:, here]], axis=0)
    new_left[...] = nn(nn(factor, coefs) * scale, stack)
    coefs_out[...] = nn(factor, jnp.concatenate([final[:, parts[0]]] + steps, axis=1)) / scale


def copy_kernel(value, out):
    out[...] = value[...]


def right_kernel(*refs):
    paths, pieces, outs = refs[:4], refs[4:-4], refs[-4:]
    rank = paths[0].shape[0]
    stack = jnp.concatenate([path[...] for path in paths], axis=0)
    part = nn(stack, jnp.concatenate([piece[...] for piece in pieces], axis=1))
    for k, out in enumerate(outs):
        out[...] = part[k * rank : (k + 1) * rank]


def collect_kernel(spots, step, own, side, near, near_side, *refs):
    outs, held = refs[:4], refs[4]
    half = own.shape[1] // 2
    odd = spots[4] == 1
    k = 0
    for first, second in ((own, side), (near, near_side)):
        part = nn_parts(step[...], jnp.concatenate([first[...], second[...]], axis=1))
        for i in range(2):
            a = part[:, i * half : (i + 1) * half]
            b = part[:, (2 + i) * half : (3 + i) * half]
            held[spots[k]] = jnp.concatenate([jnp.where(odd, b, a), jnp.where(odd, a, b)], axis=1)
            k += 1
    for k, out in enumerate(outs):
        out[...] = held[k]


def finish_kernel(coefs, tile, own, core, far, far_core, new_right):
    stack = jnp.concatenate([tile[...], own[...] + core[...], far[...] + far_core[...]], axis=0)
    new_right[...] = nn(coefs[...], stack)


def held(*shape):
    return pltpu.VMEM(shape, f32)


def call(kernel, out_shape, *operands, scalars=0, scratch=()):
    return pl.pallas_call(
        kernel,
        in_specs=[SMEM] * scalars + [VMEM] * (len(operands) - scalars),
        out_specs=jax.tree.map(lambda _: VMEM, out_shape, is_leaf=lambda v: not isinstance(v, list)),
        out_shape=out_shape,
        scratch_shapes=scratch,
        compiler_params=LIMIT,
        cost_estimate=SHORT,
    )(*operands)


def swap(value, axis, mask, members=None):
    members = range(lax.axis_size(axis)) if members is None else members
    return lax.ppermute(value, axis, [(i, i ^ mask) for i in members])


def chip_step(place, sent, top, squares, tiles, tiles_core):
    rank, width = top.shape
    core = swap(sent, "panels", 1)
    square, wide = held(rank, rank), held(rank, width)
    shapes = [square, wide, wide, square, held(2 * rank, 2 * rank)]
    return call(chip_kernel, shapes, place, sent, core, top, squares, tiles, tiles_core, scalars=1)


def gather_line(block, index, partial, tile, beside):
    ends, middle = (0, 1, 6, 7), (2, 3, 4, 5)
    is_end = (index < 2) | (index > 5)
    outward = [(2, 0), (3, 1), (4, 6), (5, 7)]

    near = swap(block, "rows", 2)
    center = swap(block, "rows", 6, middle)
    side = swap(block, "rows", 1)
    for mask in (1, 2):
        partial = partial + swap(partial, "rows", mask)
    outer = lax.ppermute(center, "rows", outward)
    near, center, side, partial, beside = lax.optimization_barrier((near, center, side, partial, beside))

    inner = swap(near, "rows", 6, middle)
    near_side = swap(near, "rows", 1)
    crossed = jnp.where(is_end, side, center)
    far_side = lax.ppermute(crossed, "rows", [(i, i ^ (6 if i in ends else 1)) for i in range(8)])
    outer, inner, near_side, far_side, partial, tile = lax.optimization_barrier(
        (outer, inner, near_side, far_side, partial, tile)
    )

    opposite = jnp.where(is_end, outer, inner)
    far = lax.ppermute(inner, "rows", outward)
    opposite_side = swap(opposite, "rows", 1)
    partial = partial + swap(partial, "rows", 4)
    tiles = jnp.stack([tile, swap(tile, "panels", 2)])
    early = [block, side, near, near_side, opposite, far_side, center]
    late = [opposite_side, far]
    return [(v, index ^ k) for v, k in zip(early, (0, 1, 2, 3, 4, 7, 6))], [
        (v, index ^ k) for v, k in zip(late, (5, 6))
    ], partial, tiles, beside


def local(panel_left, panel_right, pivot_left, pivot_right, pattern, tile_left, tile_right, sketch):
    rows = lax.axis_size("rows")
    row = lax.axis_index("rows")
    place = lax.axis_index("panels")
    count, rank, local_columns = pivot_left.shape
    columns = tile_left.shape[2]
    width = panel_left.shape[3]
    wide = held(rank, width)
    square = held(rank, rank)
    chunk = held(rank, columns)
    tile_left, tile_right = tile_left[0], tile_right[0]
    spot = place.reshape(1).astype(jnp.int32)

    sketch_here = lax.dynamic_slice_in_dim(sketch, row * local_columns, local_columns, 1)
    sketched = jnp.einsum("rb,jkb->jrk", sketch_here, pivot_left, precision=highest)
    sketch_tile = lax.dynamic_slice_in_dim(sketch, place * columns, columns, 1)
    tile_sketched = nt(sketch_tile, tile_right)
    panel = panel_left.reshape(count * rank, width)
    products = nt(panel, panel)
    routed = rows == 8 and local_columns % 128 == 0
    tile = jnp.concatenate([tile_left, tile_sketched, jnp.zeros_like(tile_sketched)], axis=1)
    if routed:
        early, late, sketched, tiles, products = gather_line(pivot_right, row, sketched, tile, products)
    else:
        sketched = lax.psum(sketched, "rows")
        tiles = jnp.stack([tile, swap(tile, "panels", 2)])

    if routed:
        inner = inner_products(panel_right, [v for v, _ in early], [s for _, s in early])
        inner, sketched, tiles = lax.optimization_barrier((inner, sketched, tiles))
        _, pivot_left, tiles = lax.optimization_barrier((late, pivot_left, tiles))
        pivot = call(copy_kernel, held(count * rank, local_columns), pivot_left.reshape(count * rank, local_columns))
        inner, pivot = lax.optimization_barrier((inner, pivot))
        opposite = swap(pivot, "rows", 4)
        inner = inner_products(panel_right, [v for v, _ in late], [s for _, s in late], inner)
    else:
        full = lax.all_gather(pivot_right, "rows", axis=2, tiled=True)
        inner = inner_products(panel_right, [full], [jnp.int32(0)])
    tiles_core = swap(tiles, "panels", 1)

    path, whole = call(
        tree_kernel,
        [held(rank, count * rank), held(rank, (count + 1) * rank)],
        pattern,
        sketched,
        inner,
        products,
        scalars=1,
    )
    top, sent, squares = pl.pallas_call(
        top_kernel,
        in_specs=[VMEM, pl.BlockSpec(memory_space=pl.ANY)],
        out_specs=[VMEM] * 3,
        out_shape=[wide, wide, held(rank, 2 * rank)],
        scratch_shapes=[pltpu.VMEM(panel.shape, f32), pltpu.SemaphoreType.DMA],
        compiler_params=ROOMY,
        cost_estimate=SHORT,
    )(whole, panel)
    if routed:
        pieces = [pivot, opposite]
        paths = [path] + [swap(path, "rows", mask) for mask in (1, 2, 3)]
        half = held(rank, 2 * local_columns)
        paths, pieces, sent = lax.optimization_barrier((paths, pieces, sent))
        far = swap(sent, "panels", 2)
        step, near, whole_tile, tile_sketched, gram = chip_step(spot, sent, top, squares, tiles, tiles_core)
        mine, *given = call(right_kernel, [half] * 4, *paths, *pieces)
        got = [mine] + [swap(v, "rows", mask) for mask, v in zip((1, 2, 3), given)]
        depth = row // 2
        spots = jnp.stack([depth ^ place, depth ^ 2 ^ place, depth ^ 1 ^ place, depth ^ 3 ^ place, row % 2])
        parts = call(collect_kernel, [chunk] * 4, spots.astype(jnp.int32), step, *got, scalars=1, scratch=[pltpu.VMEM((4, rank, columns), f32)])
        far, own_part = lax.optimization_barrier((far, parts[0]))
        rights = [own_part] + [swap(parts[mask], "panels", mask) for mask in (1, 2, 3)]
    else:
        step, near, whole_tile, tile_sketched, gram = chip_step(spot, sent, top, squares, tiles, tiles_core)
        far = swap(sent, "panels", 2)
        full_left = lax.all_gather(pivot_left, "rows", axis=2, tiled=True)
        right = nn(step, nn(path, full_left.reshape(count * rank, width)))
        rights = []
        for mask in range(4):
            part = lax.dynamic_slice_in_dim(right, (place ^ mask) * columns, columns, 1)
            rights.append(swap(part, "panels", mask) if mask else part)

    far_core = swap(far, "panels", 1)
    new_left, coefs = call(
        root_kernel,
        [jax.ShapeDtypeStruct((rank, columns), f32), held(rank, 3 * rank)],
        spot,
        near,
        far,
        far_core,
        whole_tile,
        gram,
        tile_sketched,
        scalars=1,
    )
    new_right = call(finish_kernel, jax.ShapeDtypeStruct((rank, columns), f32), coefs, tile_right, *rights)
    return (new_left[None], new_right[None])


def solution(mesh):
    return jax.shard_map(
        local,
        mesh=mesh,
        in_specs=(
            P("rows", "panels", None, None),
            P("rows", "panels", None, None),
            P("panels", None, "rows"),
            P("panels", None, "rows"),
            P("rows", "panels"),
            P("rows", None, "panels"),
            P("rows", None, "panels"),
            P(),
        ),
        out_specs=(P("rows", None, "panels"), P("rows", None, "panels")),
        check_vma=False,
    )
```
